32 devices in a mesh: axial: 8 (over z, x), cross: 4 (over y, core).
Axes of the slice: x: 2, y: 2, z: 4, core: 2. Of those that a mesh axis runs over, the one named last changes fastest.
Arguments:
- cotangent: float32 [128, 32, 16, 128], P('axial', None, 'cross'), may hold values from -8 to 8
- diag_blocks: float32 [128, 32, 32], P('axial'), as said below
- lower_rates: float32 [128, 32], P('axial'), as said below
- upper_rates: float32 [128, 32], P('axial'), as said below
- cross_rate: float32 [32], replicated, may hold values from 0.02 to 0.24
- bin_profile: float32 [32], replicated, may hold values from 0.1 to 1
- open_cells: int32 [16, 128], replicated, may hold values 0 or 1
- segment_ids: int32 [128, 16], P('axial', 'cross'), may hold values from 0 to 127
Outputs:
- grad_state: float32 [128, 32, 16, 128], P('axial', None, 'cross')
- grad_emission: float32 [128], P(('axial', 'cross'))
The draws below stay inside these ranges and needn't reach their ends.
Inputs may be any that keep to these rules, and one draw needn't show every extreme that they name: In every row (i, b) of the forward operator, diag_blocks[i, b, b] exceeds lower_rates[i, b] + upper_rates[i, b] + the sum of the magnitudes of the other entries of diag_blocks[i, b, :] by 1 or more. `lower_rates`: Positive. `upper_rates`: Positive.
All inputs are finite; a program needn't handle non-finite values.
Results may differ from the reference program's by a relative error of at most 0.0003.
Values sent between devices are 32-bit elements; how exact they have to be, the bound alone decides.
A program may use at most 64 MiB of HBM per device.

```python
import math
import jax
import jax.numpy as jnp
from jax import lax

B = 32
CA = 16
Y_DEV = 4
NZ = 128
AXIAL_CELLS = 128
NY = 16
SEGMENTS = 128
N_CROSS = 4


def spread(key, shape, low_end, high_end):
    return jnp.exp(jax.random.uniform(key, shape, jnp.float32, math.log(low_end), math.log(high_end)))


def operator_law(key):
    base_key = jax.random.fold_in(key, 41)
    random_key_list = jax.random.split(base_key, 10)
    slow_share = 0.5
    slow_low = 0.04
    slow_high = 0.25
    slow_bins = jax.random.uniform(random_key_list[0], (B,), jnp.float32) < slow_share
    square_span = float(8 * CA * (8 * CA))
    bin_rate = jnp.where(slow_bins, square_span * spread(random_key_list[1], (B,), slow_low, slow_high), spread(random_key_list[2], (B,), 0.3, 3.0))
    settled_dust = jnp.where(slow_bins, spread(random_key_list[3], (B,), 0.05, 0.5), spread(random_key_list[4], (B,), 0.5, 3.0))
    block_factor = jnp.repeat(spread(random_key_list[5], (AXIAL_CELLS // CA,), 0.6, 1.6), CA)
    cell_scale = bin_rate[None, :] * block_factor[:, None]
    lower_side_rates = cell_scale * jax.random.uniform(random_key_list[6], (AXIAL_CELLS, B), jnp.float32, 0.5, 1.5)
    upper_side_rates = cell_scale * jax.random.uniform(random_key_list[7], (AXIAL_CELLS, B), jnp.float32, 0.5, 1.5)
    spike_cells = (jax.random.uniform(random_key_list[8], (AXIAL_CELLS,), jnp.float32) < 4.0 / AXIAL_CELLS).astype(jnp.float32)
    safety_margin = (1.0 + settled_dust)[None, :] + spike_cells[:, None] * 0.5 * (lower_side_rates + upper_side_rates)
    off_diag = 1.0 - jnp.eye(B, dtype=jnp.float32)
    bin_coupling = jax.random.uniform(random_key_list[9], (AXIAL_CELLS, B, B), jnp.float32, -1.0, 1.0) * (0.5 / (B - 1)) * (1.0 + settled_dust)[None, :, None] * off_diag
    centre = safety_margin + 0.5 * (1.0 + settled_dust)[None, :] + lower_side_rates + upper_side_rates
    blocks = bin_coupling + centre[:, :, None] * jnp.eye(B, dtype=jnp.float32)[None, :, :]
    return (blocks, lower_side_rates, upper_side_rates)


def draw_diag_blocks(key, part):
    return operator_law(key)[0]


def draw_lower_rates(key, part):
    return operator_law(key)[1]


def draw_upper_rates(key, part):
    return operator_law(key)[2]


def draw_cotangent(key, part):
    base_key = jax.random.fold_in(key, 73)
    random_key_list = jax.random.split(base_key, 5)
    axial_pos = (jnp.arange(AXIAL_CELLS, dtype=jnp.float32) + 0.5) / AXIAL_CELLS
    wave_phase = jax.random.uniform(random_key_list[1], (B,), jnp.float32, 0.0, 2.0 * math.pi)
    wave_count = jax.random.uniform(random_key_list[2], (B,), jnp.float32, 0.5, 2.5)
    cross_factor = jax.random.uniform(random_key_list[3], (NY, NZ), jnp.float32, 0.5, 1.5)
    rough_part = jax.random.normal(random_key_list[0], (AXIAL_CELLS, B, NY, NZ), jnp.float32)
    smooth_level = jax.random.uniform(random_key_list[4], (B,), jnp.float32, -1.0, 1.0)
    along_line = smooth_level[None, :] * (1.0 + 0.6 * jnp.sin(2.0 * math.pi * wave_count[None, :] * axial_pos[:, None] + wave_phase[None, :]))
    whole_field = rough_part + along_line[:, :, None, None] * cross_factor[None, None, :, :]
    return jnp.clip(whole_field, -8.0, 8.0)


def touch_ends(result, own_key, least, high):
    shape = result.shape
    place = [jax.random.randint(jax.random.fold_in(own_key, axis), (), 0, shape[axis]) for axis in range(len(shape))]
    result = result.at[tuple(place)].set(least)
    longest = shape.index(max(shape))
    place[longest] = (place[longest] + 1) % shape[longest]
    return result.at[tuple(place)].set(high)


def setup_inputs(seed: int = 0) -> dict:
    splits = jax.random.split(jax.random.key(seed), 9)
    cotangent = draw_cotangent(jax.random.fold_in(splits[8], 71), 0)
    diag_blocks = draw_diag_blocks(jax.random.fold_in(splits[8], 71), 0)
    lower_rates = draw_lower_rates(jax.random.fold_in(splits[8], 71), 0)
    upper_rates = draw_upper_rates(jax.random.fold_in(splits[8], 71), 0)
    cross_rate = jnp.clip(jax.random.uniform(splits[4], (B,), jnp.float32, 0.02, 0.24), 0.02, 0.24)
    bin_profile = jnp.clip(jnp.exp(jax.random.uniform(splits[5], (B,), jnp.float32, math.log(0.1), math.log(1.0))), 0.1, 1.0)
    open_cells = touch_ends((jax.random.randint(splits[6], (NY, NZ), 0, 8) < 7).astype(jnp.int32), jax.random.fold_in(splits[6], 1), 0, 1)
    segment_ids = touch_ends(jax.random.randint(splits[7], (AXIAL_CELLS, NY), 0, SEGMENTS), jax.random.fold_in(splits[7], 1), 0, SEGMENTS - 1).astype(jnp.int32)
    return {"cotangent": cotangent, "diag_blocks": diag_blocks, "lower_rates": lower_rates, "upper_rates": upper_rates, "cross_rate": cross_rate, "bin_profile": bin_profile, "open_cells": open_cells, "segment_ids": segment_ids}


exact_precision = lax.Precision.HIGHEST

def solve_lines(right_side, below_rate, above_rate, adjoint_diag):
    bin_count = right_side.shape[1]
    zero_row = jnp.zeros((1, bin_count), jnp.float32)
    c_prev = jnp.concatenate([zero_row, above_rate[:-1]], axis=0)

    def forward(state_carry, inputs):
        inverse_prev, solve_prev = state_carry
        a_vec, c_last, diag_block, source = inputs
        weight = a_vec[:, None] * inverse_prev
        inverse_now = jnp.linalg.inv(diag_block - weight * c_last[None, :])
        solve_now = source - jnp.matmul(weight, solve_prev, precision=exact_precision)
        return ((inverse_now, solve_now), (inverse_now, solve_now))
    start_state = (jnp.zeros((bin_count, bin_count), jnp.float32), jnp.zeros(right_side.shape[1:], jnp.float32))
    _, (inverses, solves) = lax.scan(forward, start_state, (below_rate, c_prev, adjoint_diag, right_side))

    def backward(next_value, inputs):
        inverse_now, solve_now, c_vec = inputs
        value = jnp.matmul(inverse_now, solve_now - c_vec[:, None] * next_value, precision=exact_precision)
        return (value, value)
    _, values = lax.scan(backward, jnp.zeros(right_side.shape[1:], jnp.float32), (inverses, solves, above_rate), reverse=True)
    return values

def reference(cotangent, diag_blocks, lower_rates, upper_rates, cross_rate, bin_profile, open_cells, segment_ids):
    axial_total, bin_count, rows_all, depth_all = cotangent.shape
    zero_row = jnp.zeros((1, bin_count), jnp.float32)
    below_rate = -jnp.concatenate([zero_row, upper_rates[:-1]], axis=0)
    above_rate = -jnp.concatenate([lower_rates[1:], zero_row], axis=0)
    adjoint_diag = jnp.swapaxes(diag_blocks, 1, 2)
    line_tiles = cotangent.reshape(axial_total, bin_count, N_CROSS, Y_DEV * depth_all)
    line_tiles = jnp.transpose(line_tiles, (2, 0, 1, 3))
    solved = lax.map(lambda tile: solve_lines(tile, below_rate, above_rate, adjoint_diag), line_tiles)
    adjoint = jnp.transpose(solved, (1, 2, 0, 3)).reshape(axial_total, bin_count, rows_all, depth_all)
    open_mask = open_cells.astype(jnp.float32)
    mask_pad = jnp.pad(open_mask, 1)
    field_pad = jnp.pad(adjoint, ((0, 0), (0, 0), (1, 1), (1, 1)))
    flux_sum = jnp.zeros_like(adjoint)
    for shift_y, shift_z in ((0, 1), (2, 1), (1, 0), (1, 2)):
        neighbour_mask = mask_pad[shift_y:shift_y + rows_all, shift_z:shift_z + depth_all]
        neighbour = field_pad[:, :, shift_y:shift_y + rows_all, shift_z:shift_z + depth_all]
        flux_sum = flux_sum + neighbour_mask * (neighbour - adjoint)
    grad_state = adjoint + cross_rate[None, :, None, None] * open_mask * flux_sum
    emitted = jnp.einsum('ibyz,yz->iby', adjoint, open_mask, precision=exact_precision)
    emitted = jnp.einsum('iby,b->iy', emitted, bin_profile, precision=exact_precision) / depth_all
    grad_emission = jax.ops.segment_sum(emitted.reshape(-1), segment_ids.reshape(-1), num_segments=SEGMENTS)
    return (grad_state, grad_emission)
```

```python
import functools

import jax
import jax.numpy as jnp
from jax import lax
from jax.experimental import pallas as pl
from jax.experimental.pallas import tpu as pltpu
from jax.sharding import PartitionSpec as P

SEG_DEV = 4
MESH = pl.DeviceIdType.MESH
exact = lax.Precision.HIGHEST


def dot(a, b):
    return jnp.dot(a, b, precision=exact, preferred_element_type=jnp.float32)


def halves(x):
    high = x.astype(jnp.bfloat16)
    return high, (x - high.astype(jnp.float32)).astype(jnp.bfloat16)


def dot_halves(a, b):
    (ah, al), (bh, bl) = a, b
    one = functools.partial(jnp.dot, preferred_element_type=jnp.float32)
    return one(ah, bh) + (one(ah, bl) + one(al, bh))


def dot_split(a, b):
    return dot_halves(a, halves(b))


def dot3(a, b):
    return dot_halves(halves(a), halves(b))


def dot_split_b(a, b):
    return dot_halves(halves(a), b)


def spread(x, k, nb):
    packs, height, width = x.shape
    flat = x.reshape(packs * height, width)
    lane = lax.broadcasted_iota(jnp.int32, flat.shape, 1)
    return jnp.take_along_axis(flat, lane // nb * nb + k, axis=1).reshape(x.shape)


def invert_packs(a, nb):
    packs, _, width = a.shape
    row_id = lax.broadcasted_iota(jnp.int32, (packs, 8, width), 1)
    for first in range(0, nb, 8):
        home = a[:, first : first + 8]
        rest = [x for x in (a[:, :first], a[:, first + 8 :]) if x.shape[1]]
        rest = jnp.concatenate(rest, axis=1) if len(rest) > 1 else rest[0]
        near = [spread(home, first + j, nb) for j in range(8)]
        far = [spread(rest, first + j, nb) for j in range(8)]
        at = lax.broadcasted_iota(jnp.int32, home.shape, 2) % nb - first
        home = jnp.where((at >= 0) & (at < 8), jnp.where(at == row_id, 1.0, 0.0), home)
        at = lax.broadcasted_iota(jnp.int32, rest.shape, 2) % nb - first
        rest = jnp.where((at >= 0) & (at < 8), 0.0, rest)
        for j in range(8):
            pivot = 1.0 / jnp.broadcast_to(near[j][:, j : j + 1], home.shape)
            row = jnp.broadcast_to(home[:, j : j + 1], home.shape) * pivot
            home = jnp.where(row_id == j, row, home - near[j] * row)
            for m in range(j + 1, 8):
                entry = jnp.broadcast_to(near[m][:, j : j + 1], home.shape) * pivot
                near[m] = jnp.where(row_id == j, entry, near[m] - near[j] * entry)
        for j in range(8):
            rest = rest - far[j] * home[:, j : j + 1]
        a = jnp.concatenate([x for x in (rest[:, :first], home, rest[:, first:]) if x.shape[1]], axis=1)
    return a


def invert(mats):
    nb = mats[0].shape[0]
    pack = 128 // nb
    padded = list(mats)
    while len(padded) % pack:
        padded.append(mats[len(padded) % len(mats)])
    packs = [jnp.concatenate(padded[i : i + pack], axis=1) for i in range(0, len(padded), pack)]
    done = invert_packs(jnp.stack(packs), nb)
    return [done[i // pack, :, i % pack * nb : (i % pack + 1) * nb] for i in range(len(mats))]


def kernel(n, nc, cot_hbm, diag_hbm, low_hbm, up_hbm, cross_hbm, prof_hbm, open_hbm, seg_hbm, out, out_seg, GH, GL, FH, FL,
           cot, diag, low, up, cross_rate, prof_rate, open_ref, seg, G, F, X, V, port_out, port_in, msg_out, msg_in, back_out, back_in,
           edge_out, edge_in, sum_out, sum_cross, sum_axial, s_in, s_port, r_port, s_msg, r_msg, s_back, r_back, s_hal, r_hal,
           s_edge, r_edge, s_cross, r_cross, s_axial, r_axial):
    pairs_in = [(cot_hbm, cot), (diag_hbm, diag), (low_hbm, low), (up_hbm, up), (cross_hbm, cross_rate), (prof_hbm, prof_rate),
                (open_hbm, open_ref), (seg_hbm, seg)]
    loads = [pltpu.make_async_copy(src, dst, s_in.at[i]) for i, (src, dst) in enumerate(pairs_in)]
    for i in (1, 0, 2, 3, 4, 5, 6, 7):
        loads[i].start()
    cells, nb = diag.shape[0], diag.shape[1]
    size = cells * nb
    rows = cot.shape[0] // size
    nz = cot.shape[1]
    per = rows * nz // n
    a = lax.axis_index("axial")
    c = lax.axis_index("cross")
    has_lo = c > 0
    has_hi = c < nc - 1

    barrier = pltpu.get_barrier_semaphore()
    for off in range(1, n):
        pl.semaphore_signal(barrier, inc=1, device_id=(lax.rem(a + off, n), c), device_id_type=MESH)

    for off in range(1, nc):
        pl.semaphore_signal(barrier, inc=1, device_id=(a, lax.rem(c + off, nc)), device_id_type=MESH)

    for i in range(2, 8):
        loads[i].wait()
    V[...] = jnp.zeros(V.shape, jnp.float32)
    V[0:cells, 0:nb] = low[...]
    V[cells : 2 * cells, 0:nb] = up[...]
    V[2 * cells : 2 * cells + 1, 0:nb] = cross_rate[...]
    V[2 * cells + 2 : 2 * cells + 2 + rows, 0:cells] = seg[...].astype(jnp.float32)
    V[...] = V[...].T
    low_col = [V[0:nb, j : j + 1] for j in range(cells)]
    up_col = [V[0:nb, cells + j : cells + j + 1] for j in range(cells)]
    cross_col = V[0:nb, 2 * cells : 2 * cells + 1]
    seg_col = [V[0:cells, 2 * cells + 2 + y : 2 * cells + 3 + y] for y in range(rows)]
    eye = (lax.broadcasted_iota(jnp.int32, (nb, nb), 0) == lax.broadcasted_iota(jnp.int32, (nb, nb), 1)).astype(jnp.float32)

    loads[1].wait()
    pack = 128 // nb
    inverses = invert_packs(
        jnp.stack([jnp.concatenate([diag[g * pack + i] for i in range(pack)], axis=1) for g in range(cells // pack)]), nb)
    tall = [inverses[g].T for g in range(cells // pack)]

    loads[0].wait()
    for y in range(rows):
        F[:, (y + 1) * nz : (y + 2) * nz] = cot[pl.ds(y, size, stride=rows), :]
    main = slice(nz, (rows + 1) * nz)

    pl.semaphore_wait(barrier, n - 1 + nc - 1)

    def hal_copy(down):
        src = F.at[:, nz : 2 * nz] if down else F.at[:, rows * nz : (rows + 1) * nz]
        dst = F.at[:, (rows + 1) * nz : (rows + 2) * nz] if down else F.at[:, 0:nz]
        way = 0 if down else 1
        return pltpu.make_async_remote_copy(
            src_ref=src, dst_ref=dst, send_sem=s_hal.at[way], recv_sem=r_hal.at[way],
            device_id=(a, c - 1 if down else c + 1), device_id_type=MESH)

    def edge_copy(down):
        way = 0 if down else 1
        return pltpu.make_async_remote_copy(
            src_ref=edge_out.at[way], dst_ref=edge_in.at[way], send_sem=s_edge.at[way], recv_sem=r_edge.at[way],
            device_id=(a, c - 1 if down else c + 1), device_id_type=MESH)

    @pl.when(has_lo)
    def _():
        hal_copy(True).start()

    @pl.when(has_hi)
    def _():
        hal_copy(False).start()

    @pl.when(jnp.logical_not(has_lo))
    def _():
        F[:, 0:nz] = jnp.zeros((size, nz), jnp.float32)

    @pl.when(jnp.logical_not(has_hi))
    def _():
        F[:, (rows + 1) * nz : (rows + 2) * nz] = jnp.zeros((size, nz), jnp.float32)

    FH[:, main], FL[:, main] = halves(F[:, main])

    groups = []
    for i in range(cells):
        one = tall[i // pack][i % pack * nb : (i % pack + 1) * nb]
        groups.append(jnp.concatenate([low_col[i] * one, up_col[i] * one], axis=0))
    levels = []
    while len(groups) > 1:
        pairs = [(groups[i], groups[i + 1]) for i in range(0, len(groups), 2)]
        width = groups[0].shape[1]
        none = jnp.zeros((nb, width), jnp.float32)
        meets = [dot(r[:, 0:nb], l[nb:]) for l, r in pairs]
        weights = invert([eye - k[:nb, width - nb :] for k in meets])
        level = []
        groups = []
        for (l, r), k, w in zip(pairs, meets, weights):
            p = dot(w, jnp.concatenate([k[:nb], r[:nb]], axis=1))
            base = jnp.concatenate([jnp.concatenate([l[:nb], none], axis=1), jnp.concatenate([k[nb:], r[nb:]], axis=1)], axis=0)
            groups.append(base + dot(jnp.concatenate([l[:nb, width - nb :], k[nb:, width - nb :]], axis=0), p))
            level.append(p)
        levels.append(level)

    ends = groups[0]
    ports = jnp.concatenate([ends[:, 0:nb], ends[:, size - nb : size]], axis=1)
    port_out[...] = jnp.concatenate([ports[:nb], ports[nb:]], axis=1)

    def port_copy(off):
        peer = lax.rem(a + off, n)
        return pltpu.make_async_remote_copy(
            src_ref=port_out, dst_ref=port_in.at[a], send_sem=s_port.at[off], recv_sem=r_port.at[off],
            device_id=(peer, c), device_id_type=MESH)

    def msg_copy(off):
        peer = lax.rem(a + off, n)
        return pltpu.make_async_remote_copy(
            src_ref=msg_out.at[peer], dst_ref=msg_in.at[a], send_sem=s_msg.at[off], recv_sem=r_msg.at[off],
            device_id=(peer, c), device_id_type=MESH)

    def back_copy(off):
        peer = lax.rem(a + off, n)
        return pltpu.make_async_remote_copy(
            src_ref=back_out.at[peer], dst_ref=back_in.at[a], send_sem=s_back.at[off], recv_sem=r_back.at[off],
            device_id=(peer, c), device_id_type=MESH)

    for off in range(1, n):
        port_copy(off).start()
    port_in[a] = port_out[...]
    field = dot_split_b(ends, (FH[:, main], FL[:, main]))
    for e in range(n):
        bits = [field[:nb, e * per : (e + 1) * per], field[nb:, e * per : (e + 1) * per]]
        if per < 64:
            blank = jnp.zeros((nb, 64 - per), jnp.float32)
            bits = [bits[0], blank, bits[1], blank]
        msg_out[e] = jnp.concatenate(bits, axis=1)
    for off in range(1, n):
        msg_copy(off).start()
    msg_in[a] = msg_out[a]

    G[...] = jnp.zeros(G.shape, jnp.float32)
    same = (lax.broadcasted_iota(jnp.int32, (128, 128), 0) // nb) == (lax.broadcasted_iota(jnp.int32, (128, 128), 1) // nb)
    for g in range(cells // pack):
        G[g * 128 : (g + 1) * 128, g * 128 : (g + 1) * 128] = jnp.where(same, jnp.concatenate([tall[g]] * pack, axis=1), 0.0)
    width = nb
    for level in levels:
        span = max(128, 2 * width)
        for i, p in enumerate(level):
            o, m = 2 * i * width, (2 * i + 1) * width
            lo = o // span * span
            if span > 2 * width:
                blank = [jnp.zeros((nb, x), jnp.float32) for x in (o - lo, lo + span - o - 2 * width)]
                p = jnp.concatenate([x for x in (blank[0], p, blank[1]) if x.shape[1]], axis=1)
            left = G[o:m, lo : lo + span] + dot3(G[o:m, m - nb : m], p)
            G[m : m + width, lo : lo + span] += dot3(G[m : m + width, m : m + nb], up_col[m // nb - 1] * left[width - nb :])
            G[o:m, lo : lo + span] = left
        width *= 2

    half = rows * nz // 2
    GH[...], GL[...] = halves(G[...])
    for part in range(2):
        at = slice(nz + part * half, nz + (part + 1) * half)
        X[:, at] = dot_halves((GH[...], GL[...]), (FH[:, at], FL[:, at]))

    for off in range(1, n):
        port_copy(off).wait_recv()

    lane = lax.broadcasted_iota(jnp.int32, (1, 128), 1)
    keep_l = jnp.where((lane >= nb) & (lane < 2 * nb), 0.0, 1.0)
    keep_r = jnp.where(lane < nb, 0.0, 1.0)
    field_in = None
    groups = [(port_in[d][:, 0 : 2 * nb], port_in[d][:, 2 * nb :], None) for d in range(n)]
    while len(groups) > 1:
        pairs = [(groups[i], groups[i + 1]) for i in range(0, len(groups), 2)]
        meets = [dot(r[0][:, 0:nb], l[1][:, nb : 2 * nb]) for l, r in pairs]
        weights = invert([eye - k for k in meets])
        if field_in is None:
            for off in range(1, n):
                msg_copy(off).wait_recv()
            field_in = [msg_in[d] for d in range(n)]
            groups = [(jnp.concatenate([f[:, 0 : 2 * nb], h[:, 0:64]], axis=1), jnp.concatenate([t, h[:, 64:]], axis=1), None)
                      for (f, t, _), h in zip(groups, field_in)]
            pairs = [(groups[i], groups[i + 1]) for i in range(0, len(groups), 2)]
        rights = [jnp.concatenate(r[0:2] if r[2] is None else r, axis=0) for l, r in pairs]
        meets = [dot(r[:, 0:nb], l[1]) for (l, _), r in zip(pairs, rights)]
        groups = []
        for (l, _), r, k, w in zip(pairs, rights, meets, weights):
            p = dot(w, k[:nb] * keep_l + r[:nb] * keep_r)
            left = jnp.concatenate([l[0], l[1]] if l[2] is None else [l[0], l[2], l[1]], axis=0)
            base = jnp.concatenate([left * keep_l, k[nb:] * keep_l + r[nb:] * keep_r], axis=0)
            both = base + dot(jnp.concatenate([left[:, nb : 2 * nb], k[nb:, nb : 2 * nb]], axis=0), p)
            seam = left.shape[0]
            inner = [both[nb : seam - nb], p, both[seam - nb : seam], both[seam + nb :]]
            groups.append((both[:nb], both[seam : seam + nb], jnp.concatenate([x for x in inner if x.shape[0]], axis=0)))
    inner = groups[0][2]
    none = jnp.zeros((nb, 64), jnp.float32)
    for d in range(n):
        sides = [inner[(2 * d - 1) * nb : 2 * d * nb, 2 * nb :] if d > 0 else none,
                 inner[2 * d * nb : (2 * d + 1) * nb, 2 * nb :] if d < n - 1 else none]
        back_out[d] = jnp.concatenate(sides, axis=1)
    for off in range(1, n):
        back_copy(off).start()
    back_in[a] = back_out[a]

    @pl.when(has_lo)
    def _():
        hal_copy(True).wait_send()
        hal_copy(False).wait_recv()

    @pl.when(has_hi)
    def _():
        hal_copy(False).wait_send()
        hal_copy(True).wait_recv()

    sides = dot_split((GH[...], GL[...]), jnp.concatenate([F[:, 0:nz], F[:, (rows + 1) * nz : (rows + 2) * nz]], axis=1))
    X[:, 0:nz] = sides[:, 0:nz]
    X[:, (rows + 1) * nz : (rows + 2) * nz] = sides[:, nz : 2 * nz]

    sent = jnp.concatenate([prof_rate[...]] * cells, axis=1)
    mine = lax.broadcasted_iota(jnp.int32, (cells, size), 1) // nb == lax.broadcasted_iota(jnp.int32, (cells, size), 0)
    sent = dot_halves(halves(jnp.where(mine, sent, 0.0)), (GH[...], GL[...]))
    emit = dot_split_b(sent, (FH[:, main], FL[:, main]))
    sent = jnp.concatenate([sent[:, 0:nb], sent[:, size - nb : size]], axis=1)

    for off in range(1, n):
        back_copy(off).wait_recv()

    each = n // rows
    flux = []
    for y in range(rows):
        flux.append(jnp.concatenate([
            jnp.concatenate([back_in[y * each + e][:, at : at + per] for e in range(each)], axis=1) for at in (0, 64)], axis=0))
    edge_out[0] = flux[0]
    edge_out[1] = flux[rows - 1]

    @pl.when(has_lo)
    def _():
        edge_copy(True).start()

    @pl.when(has_hi)
    def _():
        edge_copy(False).start()

    opens = []
    for y in range(-1, rows + 1):
        at = jnp.clip(c * rows + y, 0, nc * rows - 1)
        line = open_ref[pl.ds(at, 1), :].astype(jnp.float32)
        if y == -1:
            line = jnp.where(has_lo, line, 0.0)
        if y == rows:
            line = jnp.where(has_hi, line, 0.0)
        opens.append(line)

    segs = sum_out.shape[-1]
    seg_id = lax.broadcasted_iota(jnp.int32, (1, segs), 1)
    gain = jnp.zeros((8, segs), jnp.float32)
    flux = halves(jnp.concatenate(flux, axis=1))
    emit = emit + dot_halves(halves(sent), flux)
    for y in range(rows):
        given = jnp.sum(emit[:, y * nz : (y + 1) * nz] * opens[y + 1], axis=1, keepdims=True) * (1.0 / nz)
        picked = jnp.where(seg_col[y] == seg_id.astype(jnp.float32), given, 0.0)
        for i in range(cells // 8):
            gain = gain + picked[i * 8 : (i + 1) * 8]
    sum_out[0] = gain

    def cross_copy(off):
        return pltpu.make_async_remote_copy(
            src_ref=sum_out.at[0], dst_ref=sum_cross.at[off], send_sem=s_cross.at[off], recv_sem=r_cross.at[off],
            device_id=(a, lax.rem(c + off, nc)), device_id_type=MESH)

    def axial_copy(off):
        return pltpu.make_async_remote_copy(
            src_ref=sum_out.at[1], dst_ref=sum_axial.at[off], send_sem=s_axial.at[off], recv_sem=r_axial.at[off],
            device_id=(lax.rem(a + off, n), c), device_id_type=MESH)

    for off in range(1, nc):
        cross_copy(off).start()

    gc = (jnp.concatenate([GH[:, 0:nb], GH[:, size - nb : size]], axis=1),
          jnp.concatenate([GL[:, 0:nb], GL[:, size - nb : size]], axis=1))
    X[:, main] += dot_halves(gc, flux)

    zlane = lax.broadcasted_iota(jnp.int32, (1, nz), 1)
    step_col = jnp.concatenate([cross_col] * 4, axis=0)
    block = 4 * nb
    for y in list(range(1, rows - 1)) + [0, rows - 1]:
        if y == 0:
                @pl.when(has_lo)
                def _():
                    edge_copy(True).wait_send()
                    edge_copy(False).wait_recv()
                    X[:, 0:nz] += dot_split(gc, edge_in[1])

                @pl.when(has_hi)
                def _():
                    edge_copy(False).wait_send()
                    edge_copy(True).wait_recv()
                    X[:, (rows + 1) * nz : (rows + 2) * nz] += dot_split(gc, edge_in[0])

        here = opens[y + 1]
        before = jnp.where(zlane == 0, 0.0, pltpu.roll(here, 1, 1)) * here
        after = jnp.where(zlane == nz - 1, 0.0, pltpu.roll(here, nz - 1, 1)) * here
        above = opens[y] * here
        below = opens[y + 2] * here
        total = before + after + above + below
        for i in range(size // block):
            at = slice(i * block, (i + 1) * block)
            x = X[at, (y + 1) * nz : (y + 2) * nz]
            moved = (above * (X[at, y * nz : (y + 1) * nz] - x) + below * (X[at, (y + 2) * nz : (y + 3) * nz] - x)
                     + before * (pltpu.roll(x, 1, 1) - x) + after * (pltpu.roll(x, nz - 1, 1) - x))
            out[pl.ds(i * block * rows + y, block, stride=rows), :] = x + step_col * moved
        if y == 1:
            gain = sum_out[0]
            for off in range(1, nc):
                cross_copy(off).wait_recv()
                gain = gain + sum_cross[off]
            sum_out[1] = gain
            for off in range(1, n):
                axial_copy(off).start()

    gain = sum_out[1]
    for off in range(1, n):
        axial_copy(off).wait_recv()
        gain = gain + sum_axial[off]
    gain = jnp.sum(gain, axis=0, keepdims=True)
    own = out_seg.shape[1]
    own_id = lax.broadcasted_iota(jnp.int32, (1, own), 1)
    result = jnp.zeros((1, own), jnp.float32)
    for j in range(own):
        mine = jnp.sum(jnp.where(seg_id == (a * nc + c) * own + j, gain, 0.0), axis=1, keepdims=True)
        result = jnp.where(own_id == j, mine, result)
    out_seg[...] = result

    for off in range(1, nc):
        cross_copy(off).wait_send()
    for off in range(1, n):
        axial_copy(off).wait_send()

    for off in range(1, n):
        port_copy(off).wait_send()
        msg_copy(off).wait_send()
        back_copy(off).wait_send()


def per_device(n, nc, cotangent, diag_blocks, lower_rates, upper_rates, cross_rate, bin_profile, open_cells, segment_ids):
    cells, nb, rows, nz = cotangent.shape
    size = cells * nb
    segs = SEG_DEV * n * nc
    vmem = pl.BlockSpec(memory_space=pltpu.VMEM)
    hbm = pl.BlockSpec(memory_space=pltpu.HBM)
    dma = pltpu.SemaphoreType.DMA
    f32 = jnp.float32
    operands = (
        cotangent.reshape(size * rows, nz), diag_blocks, lower_rates, upper_rates,
        cross_rate.reshape(1, nb), bin_profile.reshape(1, nb), open_cells, segment_ids.T,
    )
    operands = [pltpu.with_memory_space_constraint(x, pltpu.HBM) for x in operands]
    grad, gain = pl.pallas_call(
        functools.partial(kernel, n, nc),
        out_shape=(pltpu.VMEM((size * rows, nz), f32), jax.ShapeDtypeStruct((1, SEG_DEV), f32)),
        in_specs=[hbm] * len(operands),
        out_specs=(vmem, vmem),
        scratch_shapes=[pltpu.VMEM((size, size), jnp.bfloat16)] * 2 + [pltpu.VMEM((size, rows * nz + 2 * nz), jnp.bfloat16)] * 2 + [pltpu.VMEM(x.shape, x.dtype) for x in operands] + [
            pltpu.VMEM((size, size), f32),
            pltpu.VMEM((size, (rows + 2) * nz), f32),
            pltpu.VMEM((size, (rows + 2) * nz), f32),
            pltpu.VMEM((128, 128), f32),
            pltpu.VMEM((nb, 128), f32),
            pltpu.VMEM((n, nb, 128), f32),
            pltpu.VMEM((n, nb, 128), f32),
            pltpu.VMEM((n, nb, 128), f32),
            pltpu.VMEM((n, nb, 128), f32),
            pltpu.VMEM((n, nb, 128), f32),
            pltpu.VMEM((2, 2 * nb, nz), f32),
            pltpu.VMEM((2, 2 * nb, nz), f32),
            pltpu.VMEM((2, 8, segs), f32),
            pltpu.VMEM((nc, 8, segs), f32),
            pltpu.VMEM((n, 8, segs), f32),
            dma((len(operands),)), dma((n,)), dma((n,)), dma((n,)), dma((n,)), dma((n,)), dma((n,)), dma((2,)), dma((2,)), dma((2,)), dma((2,)),
            dma((nc,)), dma((nc,)), dma((n,)), dma((n,)),
        ],
        compiler_params=pltpu.CompilerParams(
            collective_id=0, has_side_effects=True, vmem_limit_bytes=48 * 1024 * 1024
        ),
    )(*operands)
    return grad.reshape(cotangent.shape), gain.reshape(SEG_DEV)


def solution(mesh):
    in_specs = (
        P("axial", None, "cross", None),
        P("axial", None, None),
        P("axial", None),
        P("axial", None),
        P(),
        P(),
        P(),
        P("axial", "cross"),
    )
    out_specs = (P("axial", None, "cross", None), P(("axial", "cross")))
    return jax.shard_map(
        functools.partial(per_device, mesh.shape["axial"], mesh.shape["cross"]),
        mesh=mesh, in_specs=in_specs, out_specs=out_specs, check_vma=False,
    )
```

```python
import functools

import jax
import jax.numpy as jnp
from jax import lax
from jax.experimental import pallas as pl
from jax.experimental.pallas import tpu as pltpu
from jax.sharding import PartitionSpec as P

SEG_DEV = 4
EARLY = 2
MESH = pl.DeviceIdType.MESH
exact = lax.Precision.HIGHEST


def dot(a, b):
    return jnp.dot(a, b, precision=exact, preferred_element_type=jnp.float32)


def halves(x):
    high = x.astype(jnp.bfloat16)
    return high, (x - high.astype(jnp.float32)).astype(jnp.bfloat16)


def dot_halves(a, b):
    (ah, al), (bh, bl) = a, b
    one = functools.partial(jnp.dot, preferred_element_type=jnp.float32)
    return one(ah, bh) + (one(ah, bl) + one(al, bh))


def dot_split(a, b):
    return dot_halves(a, halves(b))


def dot3(a, b):
    return dot_halves(halves(a), halves(b))


def dot_split_b(a, b):
    return dot_halves(halves(a), b)


def spread(x, k, nb):
    packs, height, width = x.shape
    flat = x.reshape(packs * height, width)
    lane = lax.broadcasted_iota(jnp.int32, flat.shape, 1)
    return jnp.take_along_axis(flat, lane // nb * nb + k, axis=1).reshape(x.shape)


def invert_packs(a, nb, by_two=False):
    packs, _, width = a.shape
    row_id = lax.broadcasted_iota(jnp.int32, (packs, 8, width), 1)
    for first in range(0, nb, 8):
        home = a[:, first : first + 8]
        rest = [x for x in (a[:, :first], a[:, first + 8 :]) if x.shape[1]]
        rest = jnp.concatenate(rest, axis=1) if len(rest) > 1 else rest[0]
        near = [spread(home, first + j, nb) for j in range(8)]
        far = [spread(rest, first + j, nb) for j in range(8)]
        at = lax.broadcasted_iota(jnp.int32, home.shape, 2) % nb - first
        home = jnp.where((at >= 0) & (at < 8), jnp.where(at == row_id, 1.0, 0.0), home)
        at = lax.broadcasted_iota(jnp.int32, rest.shape, 2) % nb - first
        rest = jnp.where((at >= 0) & (at < 8), 0.0, rest)
        for j in range(0, 8, 2) if by_two else ():
            pick = lambda x, i: jnp.broadcast_to(x[:, i : i + 1], home.shape)
            a00, a01, a10, a11 = pick(near[j], j), pick(near[j + 1], j), pick(near[j], j + 1), pick(near[j + 1], j + 1)
            pivot = 1.0 / (a00 * a11 - a01 * a10)
            a00, a01, a10, a11 = a11 * pivot, a01 * pivot, a10 * pivot, a00 * pivot
            first_col, second_col = near[j], near[j + 1]

            def step(x):
                x0, x1 = pick(x, j), pick(x, j + 1)
                y0, y1 = a00 * x0 - a01 * x1, a11 * x1 - a10 * x0
                done = x - (first_col * y0 + second_col * y1)
                return jnp.where(row_id == j, y0, jnp.where(row_id == j + 1, y1, done))

            home = step(home)
            for m in range(j + 2, 8):
                near[m] = step(near[m])
        for j in range(8) if not by_two else ():
            pivot = 1.0 / jnp.broadcast_to(near[j][:, j : j + 1], home.shape)
            row = jnp.broadcast_to(home[:, j : j + 1], home.shape) * pivot
            home = jnp.where(row_id == j, row, home - near[j] * row)
            for m in range(j + 1, 8):
                entry = jnp.broadcast_to(near[m][:, j : j + 1], home.shape) * pivot
                near[m] = jnp.where(row_id == j, entry, near[m] - near[j] * entry)
        for j in range(8):
            rest = rest - far[j] * home[:, j : j + 1]
        a = jnp.concatenate([x for x in (rest[:, :first], home, rest[:, first:]) if x.shape[1]], axis=1)
    return a


def invert(mats):
    nb = mats[0].shape[0]
    pack = 128 // nb
    padded = list(mats)
    while len(padded) % pack:
        padded.append(mats[len(padded) % len(mats)])
    packs = [jnp.concatenate(padded[i : i + pack], axis=1) for i in range(0, len(padded), pack)]
    done = invert_packs(jnp.stack(packs), nb, True)
    return [done[i // pack, :, i % pack * nb : (i % pack + 1) * nb] for i in range(len(mats))]


def kernel(n, nc, cot_hbm, diag_hbm, low_hbm, up_hbm, cross_hbm, prof_hbm, open_hbm, seg_hbm, out, out_seg, GH, GL, FH, FL,
           cot, diag, low, up, cross_rate, prof_rate, open_ref, seg, G, F, X, V, port_out, port_in, msg_out, msg_in, pair_out, pair_in, back_out, back_in,
           edge_in, gain_out, gain_in, s_in, s_port, r_port, s_pair, r_pair, s_msg, r_msg, s_back, r_back, s_hal, r_hal,
           s_edge, r_edge, s_gain, r_gain):
    pairs_in = [(cot_hbm, cot), (diag_hbm, diag), (low_hbm, low), (up_hbm, up), (cross_hbm, cross_rate), (prof_hbm, prof_rate),
                (open_hbm, open_ref), (seg_hbm, seg)]
    loads = [pltpu.make_async_copy(src, dst, s_in.at[i]) for i, (src, dst) in enumerate(pairs_in)]
    for i in (1, 0, 2, 3, 4, 5, 6, 7):
        loads[i].start()
    cells, nb = diag.shape[0], diag.shape[1]
    size = cells * nb
    rows = cot.shape[0] // size
    nz = cot.shape[1]
    a = lax.axis_index("axial")
    h = n // 2
    per = rows * nz // h
    is_left = a < h
    own = lax.rem(a, h)
    half_of = a - own
    partner = lax.rem(a + h, n)
    c = lax.axis_index("cross")
    has_lo = c > 0
    has_hi = c < nc - 1

    barrier = pltpu.get_barrier_semaphore()
    peers = [(i, j) for i in range(n) for j in range(nc) if i or j]
    for i, j in peers:
        pl.semaphore_signal(barrier, inc=1, device_id=(lax.rem(a + i, n), lax.rem(c + j, nc)), device_id_type=MESH)

    for i in range(2, 8):
        loads[i].wait()
    V[...] = jnp.zeros(V.shape, jnp.float32)
    V[0:cells, 0:nb] = low[...]
    V[cells : 2 * cells, 0:nb] = up[...]
    V[2 * cells : 2 * cells + 1, 0:nb] = cross_rate[...]
    V[2 * cells + 2 : 2 * cells + 2 + rows, 0:cells] = seg[...].astype(jnp.float32)
    V[...] = V[...].T
    low_col = [V[0:nb, j : j + 1] for j in range(cells)]
    up_col = [V[0:nb, cells + j : cells + j + 1] for j in range(cells)]
    cross_col = V[0:nb, 2 * cells : 2 * cells + 1]
    seg_col = [V[0:cells, 2 * cells + 2 + y : 2 * cells + 3 + y] for y in range(rows)]
    eye = (lax.broadcasted_iota(jnp.int32, (nb, nb), 0) == lax.broadcasted_iota(jnp.int32, (nb, nb), 1)).astype(jnp.float32)

    loads[1].wait()
    pack = 128 // nb
    inverses = invert_packs(
        jnp.stack([jnp.concatenate([diag[g * pack + i] for i in range(pack)], axis=1) for g in range(cells // pack)]), nb)
    tall = [inverses[g].T for g in range(cells // pack)]

    loads[0].wait()
    for y in range(rows):
        F[:, (y + 1) * nz : (y + 2) * nz] = cot[pl.ds(y, size, stride=rows), :]
    main = slice(nz, (rows + 1) * nz)

    pl.semaphore_wait(barrier, len(peers))

    def hal_copy(down):
        src = F.at[:, nz : 2 * nz] if down else F.at[:, rows * nz : (rows + 1) * nz]
        dst = F.at[:, (rows + 1) * nz : (rows + 2) * nz] if down else F.at[:, 0:nz]
        way = 0 if down else 1
        return pltpu.make_async_remote_copy(
            src_ref=src, dst_ref=dst, send_sem=s_hal.at[way], recv_sem=r_hal.at[way],
            device_id=(a, c - 1 if down else c + 1), device_id_type=MESH)

    each = h // rows
    sends_down = jnp.logical_and(has_lo, own < each)
    sends_up = jnp.logical_and(has_hi, own >= h - each)

    def edge_copy(down, off):
        way = 0 if down else 1
        slot = own if down else own - (h - each)
        peer = lax.rem(own + off, h)
        return pltpu.make_async_remote_copy(
            src_ref=back_out.at[peer], dst_ref=edge_in.at[way, slot], send_sem=s_edge.at[way, off], recv_sem=r_edge.at[way, slot],
            device_id=(half_of + peer, c - 1 if down else c + 1), device_id_type=MESH)

    def edge_wait(way):
        for e in range(each):
            pltpu.make_async_remote_copy(
                src_ref=back_out.at[e], dst_ref=edge_in.at[way, e], send_sem=s_edge.at[way, e], recv_sem=r_edge.at[way, e],
                device_id=(a, c + 1 if way == 0 else c - 1), device_id_type=MESH).wait_recv()

    @pl.when(has_lo)
    def _():
        hal_copy(True).start()

    @pl.when(has_hi)
    def _():
        hal_copy(False).start()

    @pl.when(jnp.logical_not(has_lo))
    def _():
        F[:, 0:nz] = jnp.zeros((size, nz), jnp.float32)

    @pl.when(jnp.logical_not(has_hi))
    def _():
        F[:, (rows + 1) * nz : (rows + 2) * nz] = jnp.zeros((size, nz), jnp.float32)

    FH[:, main], FL[:, main] = halves(F[:, main])

    groups = []
    for i in range(cells):
        one = tall[i // pack][i % pack * nb : (i % pack + 1) * nb]
        groups.append(jnp.concatenate([low_col[i] * one, up_col[i] * one], axis=0))
    levels = []
    while len(groups) > 1:
        pairs = [(groups[i], groups[i + 1]) for i in range(0, len(groups), 2)]
        width = groups[0].shape[1]
        none = jnp.zeros((nb, width), jnp.float32)
        meets = [dot(r[:, 0:nb], l[nb:]) for l, r in pairs]
        weights = invert([eye - k[:nb, width - nb :] for k in meets])
        level = [dot(w, jnp.concatenate([k[:nb], r[:nb]], axis=1)) for (l, r), k, w in zip(pairs, meets, weights)]
        groups = []
        for (l, r), k, p in zip(pairs, meets, level):
            base = jnp.concatenate([jnp.concatenate([l[:nb], none], axis=1), jnp.concatenate([k[nb:], r[nb:]], axis=1)], axis=0)
            groups.append(base + dot(jnp.concatenate([l[:nb, width - nb :], k[nb:, width - nb :]], axis=0), p))
        levels.append(level)

    ends = groups[0]
    ports = jnp.concatenate([ends[:, 0:nb], ends[:, size - nb : size]], axis=1)
    port_out[...] = jnp.concatenate([ports[:nb], ports[nb:]], axis=1)

    def port_copy(off):
        return pltpu.make_async_remote_copy(
            src_ref=port_out, dst_ref=port_in.at[own], send_sem=s_port.at[off], recv_sem=r_port.at[off],
            device_id=(half_of + lax.rem(own + off, h), c), device_id_type=MESH)

    def msg_copy(off):
        peer = lax.rem(own + off, h)
        return pltpu.make_async_remote_copy(
            src_ref=msg_out.at[peer], dst_ref=msg_in.at[own], send_sem=s_msg.at[off], recv_sem=r_msg.at[off],
            device_id=(half_of + peer, c), device_id_type=MESH)

    def pair_copy():
        return pltpu.make_async_remote_copy(
            src_ref=pair_out, dst_ref=pair_in, send_sem=s_pair.at[0], recv_sem=r_pair.at[0],
            device_id=(partner, c), device_id_type=MESH)

    def back_copy(off):
        peer = lax.rem(own + off, h)
        return pltpu.make_async_remote_copy(
            src_ref=back_out.at[peer], dst_ref=back_in.at[own], send_sem=s_back.at[off], recv_sem=r_back.at[off],
            device_id=(half_of + peer, c), device_id_type=MESH)

    for off in range(1, h):
        port_copy(off).start()
    port_in[own] = port_out[...]
    field = dot_split_b(ends, (FH[:, main], FL[:, main]))
    fill = [jnp.zeros((2 * nb, 128 - per), jnp.float32)] if per < 128 else []
    for e in range(h):
        msg_out[e] = jnp.concatenate([field[:, e * per : (e + 1) * per]] + fill, axis=1)
    for off in range(1, h):
        msg_copy(off).start()
    msg_in[own] = msg_out[own]

    G[...] = jnp.zeros(G.shape, jnp.float32)
    same = (lax.broadcasted_iota(jnp.int32, (128, 128), 0) // nb) == (lax.broadcasted_iota(jnp.int32, (128, 128), 1) // nb)
    for g in range(cells // pack):
        G[g * 128 : (g + 1) * 128, g * 128 : (g + 1) * 128] = jnp.where(same, jnp.concatenate([tall[g]] * pack, axis=1), 0.0)
    def grow(level):
        width = level[0].shape[1] // 2
        span = max(128, 2 * width)
        places = [(2 * i * width, (2 * i + 1) * width, 2 * i * width // span * span) for i in range(len(level))]
        lefts = []
        for (o, m, lo), p in zip(places, level):
            if span > 2 * width:
                blank = [jnp.zeros((nb, x), jnp.float32) for x in (o - lo, lo + span - o - 2 * width)]
                p = jnp.concatenate([x for x in (blank[0], p, blank[1]) if x.shape[1]], axis=1)
            lefts.append(G[o:m, lo : lo + span] + dot3(G[o:m, m - nb : m], p))
        for (o, m, lo), left in zip(places, lefts):
            G[m : m + width, lo : lo + span] += dot3(G[m : m + width, m : m + nb], up_col[m // nb - 1] * left[width - nb :])
            G[o:m, lo : lo + span] = left

    for level in levels[:EARLY]:
        grow(level)

    for off in range(1, h):
        port_copy(off).wait_recv()

    lane = lax.broadcasted_iota(jnp.int32, (1, 256), 1)
    keep_l = jnp.where((lane >= nb) & (lane < 2 * nb), 0.0, 1.0)
    keep_r = jnp.where(lane < nb, 0.0, 1.0)
    field_in = None
    groups = [(port_in[d][:, 0 : 2 * nb], port_in[d][:, 2 * nb :], None) for d in range(h)]
    blank = jnp.zeros((nb, 128 - 2 * nb), jnp.float32)
    while len(groups) > 1:
        pairs = [(groups[i], groups[i + 1]) for i in range(0, len(groups), 2)]
        meets = [dot(r[0][:, 0:nb], l[1][:, nb : 2 * nb]) for l, r in pairs]
        weights = invert([eye - k for k in meets])
        if field_in is None:
            for off in range(1, h):
                msg_copy(off).wait_recv()
            field_in = [msg_in[d] for d in range(h)]
            groups = [(jnp.concatenate([f, blank, x[:nb]], axis=1), jnp.concatenate([t, blank, x[nb:]], axis=1), None)
                      for (f, t, _), x in zip(groups, field_in)]
            pairs = [(groups[i], groups[i + 1]) for i in range(0, len(groups), 2)]
        rights = [jnp.concatenate(r[0:2] if r[2] is None else r, axis=0) for l, r in pairs]
        meets = [dot(r[:, 0:nb], l[1]) for (l, _), r in zip(pairs, rights)]
        flows = [dot(w, k[:nb] * keep_l + r[:nb] * keep_r) for r, k, w in zip(rights, meets, weights)]
        groups = []
        for (l, _), r, k, p in zip(pairs, rights, meets, flows):
            left = jnp.concatenate([l[0], l[1]] if l[2] is None else [l[0], l[2], l[1]], axis=0)
            base = jnp.concatenate([left * keep_l, k[nb:] * keep_l + r[nb:] * keep_r], axis=0)
            both = base + dot(jnp.concatenate([left[:, nb : 2 * nb], k[nb:, nb : 2 * nb]], axis=0), p)
            seam = left.shape[0]
            inner = [both[nb : seam - nb], p, both[seam - nb : seam], both[seam + nb :]]
            groups.append((both[:nb], both[seam : seam + nb], jnp.concatenate([x for x in inner if x.shape[0]], axis=0)))
    first, last, inner = groups[0]
    mine = jnp.where(is_left, last[:, nb : 2 * nb], first[:, 0:nb])
    mine_field = jnp.where(is_left, last[:, 128:], first[:, 128:])
    pair_out[0:nb] = mine_field
    pair_out[nb:] = jnp.concatenate([mine[s * nb // 4 : (s + 1) * nb // 4] for s in range(4)], axis=1)
    pair_copy().start()
    inner_port = jnp.where(is_left, inner[:, nb : 2 * nb], inner[:, 0:nb])
    inner_field = inner[:, 128:]

    for level in levels[EARLY:]:
        grow(level)
    GH[...], GL[...] = halves(G[...])

    pair_copy().wait_recv()
    theirs = jnp.concatenate([pair_in[nb:][:, s * nb : (s + 1) * nb] for s in range(4)], axis=0)
    both = dot(theirs, jnp.concatenate([mine_field, mine], axis=1))
    given = dot(invert([eye - both[:, 128:]])[0], pair_in[0:nb] + both[:, :128])
    inner = inner_field + dot(inner_port, given)
    for d in range(h):
        back_out[d, 0:nb] = inner[(2 * d - 1) * nb : 2 * d * nb] if d > 0 else jnp.where(is_left, 0.0, given)
        back_out[d, nb:] = inner[2 * d * nb : (2 * d + 1) * nb] if d < h - 1 else jnp.where(is_left, given, 0.0)
    for off in range(1, h):
        back_copy(off).start()
    back_in[own] = back_out[own]

    @pl.when(sends_down)
    def _():
        for off in range(h):
            edge_copy(True, off).start()

    @pl.when(sends_up)
    def _():
        for off in range(h):
            edge_copy(False, off).start()

    half = rows * nz // 2
    for part in range(2):
        at = slice(nz + part * half, nz + (part + 1) * half)
        X[:, at] = dot_halves((GH[...], GL[...]), (FH[:, at], FL[:, at]))

    @pl.when(has_lo)
    def _():
        hal_copy(True).wait_send()
        hal_copy(False).wait_recv()

    @pl.when(has_hi)
    def _():
        hal_copy(False).wait_send()
        hal_copy(True).wait_recv()

    sides = dot_split((GH[...], GL[...]), jnp.concatenate([F[:, 0:nz], F[:, (rows + 1) * nz : (rows + 2) * nz]], axis=1))
    X[:, 0:nz] = sides[:, 0:nz]
    X[:, (rows + 1) * nz : (rows + 2) * nz] = sides[:, nz : 2 * nz]

    sent = jnp.concatenate([prof_rate[...]] * cells, axis=1)
    mine = lax.broadcasted_iota(jnp.int32, (cells, size), 1) // nb == lax.broadcasted_iota(jnp.int32, (cells, size), 0)
    sent = dot_halves(halves(jnp.where(mine, sent, 0.0)), (GH[...], GL[...]))
    emit = dot_split_b(sent, (FH[:, main], FL[:, main]))
    sent = jnp.concatenate([sent[:, 0:nb], sent[:, size - nb : size]], axis=1)

    for off in range(1, h):
        back_copy(off).wait_recv()

    flux = []
    for y in range(rows):
        flux.append(jnp.concatenate([back_in[y * each + e][:, 0:per] for e in range(each)], axis=1))
    opens = []
    for y in range(-1, rows + 1):
        at = jnp.clip(c * rows + y, 0, nc * rows - 1)
        line = open_ref[pl.ds(at, 1), :].astype(jnp.float32)
        if y == -1:
            line = jnp.where(has_lo, line, 0.0)
        if y == rows:
            line = jnp.where(has_hi, line, 0.0)
        opens.append(line)

    segs = gain_out.shape[-1]
    seg_id = lax.broadcasted_iota(jnp.int32, (1, segs), 1)
    gain = jnp.zeros((8, segs), jnp.float32)
    flux = halves(jnp.concatenate(flux, axis=1))
    emit = emit + dot_halves(halves(sent), flux)
    for y in range(rows):
        given = jnp.sum(emit[:, y * nz : (y + 1) * nz] * opens[y + 1], axis=1, keepdims=True) * (1.0 / nz)
        picked = jnp.where(seg_col[y] == seg_id.astype(jnp.float32), given, 0.0)
        for i in range(cells // 8):
            gain = gain + picked[i * 8 : (i + 1) * 8]
    gain_out[0] = jnp.sum(gain, axis=0, keepdims=True)

    def gain_copy(k):
        i, j = peers[k]
        return pltpu.make_async_remote_copy(
            src_ref=gain_out.at[0], dst_ref=gain_in.at[k], send_sem=s_gain.at[0], recv_sem=r_gain.at[0],
            device_id=(lax.rem(a + i, n), lax.rem(c + j, nc)), device_id_type=MESH)

    for k in range(len(peers)):
        gain_copy(k).start()

    gc = (jnp.concatenate([GH[:, 0:nb], GH[:, size - nb : size]], axis=1),
          jnp.concatenate([GL[:, 0:nb], GL[:, size - nb : size]], axis=1))
    X[:, main] += dot_halves(gc, flux)

    zlane = lax.broadcasted_iota(jnp.int32, (1, nz), 1)
    step_col = jnp.concatenate([cross_col] * 4, axis=0)
    block = 4 * nb
    for y in list(range(1, rows - 1)) + [0, rows - 1]:
        if y == 0:
                @pl.when(has_lo)
                def _():
                    edge_wait(1)
                    X[:, 0:nz] += dot_split(gc, jnp.concatenate([edge_in[1, e][:, 0:per] for e in range(each)], axis=1))

                @pl.when(has_hi)
                def _():
                    edge_wait(0)
                    X[:, (rows + 1) * nz : (rows + 2) * nz] += dot_split(
                        gc, jnp.concatenate([edge_in[0, e][:, 0:per] for e in range(each)], axis=1))

        here = opens[y + 1]
        before = jnp.where(zlane == 0, 0.0, pltpu.roll(here, 1, 1)) * here
        after = jnp.where(zlane == nz - 1, 0.0, pltpu.roll(here, nz - 1, 1)) * here
        above = opens[y] * here
        below = opens[y + 2] * here
        total = before + after + above + below
        for i in range(size // block):
            at = slice(i * block, (i + 1) * block)
            x = X[at, (y + 1) * nz : (y + 2) * nz]
            moved = (above * (X[at, y * nz : (y + 1) * nz] - x) + below * (X[at, (y + 2) * nz : (y + 3) * nz] - x)
                     + before * (pltpu.roll(x, 1, 1) - x) + after * (pltpu.roll(x, nz - 1, 1) - x))
            out[pl.ds(i * block * rows + y, block, stride=rows), :] = x + step_col * moved

    pltpu.make_async_copy(gain_in, gain_in, r_gain.at[0]).wait()
    gain = gain_out[0] + jnp.sum(gain_in[...], axis=0)
    held = out_seg.shape[1]
    held_id = lax.broadcasted_iota(jnp.int32, (1, held), 1)
    result = jnp.zeros((1, held), jnp.float32)
    for j in range(held):
        picked = jnp.sum(jnp.where(seg_id == (a * nc + c) * held + j, gain, 0.0), axis=1, keepdims=True)
        result = jnp.where(held_id == j, picked, result)
    out_seg[...] = result

    pltpu.make_async_copy(gain_in, gain_in, s_gain.at[0]).wait()

    @pl.when(sends_down)
    def _():
        for off in range(h):
            edge_copy(True, off).wait_send()

    @pl.when(sends_up)
    def _():
        for off in range(h):
            edge_copy(False, off).wait_send()

    pair_copy().wait_send()
    for off in range(1, h):
        port_copy(off).wait_send()
        msg_copy(off).wait_send()
        back_copy(off).wait_send()


def per_device(n, nc, cotangent, diag_blocks, lower_rates, upper_rates, cross_rate, bin_profile, open_cells, segment_ids):
    cells, nb, rows, nz = cotangent.shape
    size, h = cells * nb, n // 2
    segs = SEG_DEV * n * nc
    vmem = pl.BlockSpec(memory_space=pltpu.VMEM)
    hbm = pl.BlockSpec(memory_space=pltpu.HBM)
    dma = pltpu.SemaphoreType.DMA
    f32 = jnp.float32
    operands = (
        cotangent.reshape(size * rows, nz), diag_blocks, lower_rates, upper_rates,
        cross_rate.reshape(1, nb), bin_profile.reshape(1, nb), open_cells, segment_ids.T,
    )
    operands = [pltpu.with_memory_space_constraint(x, pltpu.HBM) for x in operands]
    grad, gain = pl.pallas_call(
        functools.partial(kernel, n, nc),
        out_shape=(pltpu.VMEM((size * rows, nz), f32), jax.ShapeDtypeStruct((1, SEG_DEV), f32)),
        in_specs=[hbm] * len(operands),
        out_specs=(vmem, vmem),
        scratch_shapes=[pltpu.VMEM((size, size), jnp.bfloat16)] * 2 + [pltpu.VMEM((size, rows * nz + 2 * nz), jnp.bfloat16)] * 2 + [pltpu.VMEM(x.shape, x.dtype) for x in operands] + [
            pltpu.VMEM((size, size), f32),
            pltpu.VMEM((size, (rows + 2) * nz), f32),
            pltpu.VMEM((size, (rows + 2) * nz), f32),
            pltpu.VMEM((128, 128), f32),
            pltpu.VMEM((nb, 128), f32),
            pltpu.VMEM((h, nb, 128), f32),
            pltpu.VMEM((h, 2 * nb, 128), f32),
            pltpu.VMEM((h, 2 * nb, 128), f32),
            pltpu.VMEM((nb + nb // 4, 128), f32),
            pltpu.VMEM((nb + nb // 4, 128), f32),
            pltpu.VMEM((h, 2 * nb, 128), f32),
            pltpu.VMEM((h, 2 * nb, 128), f32),
            pltpu.VMEM((2, h // rows, 2 * nb, 128), f32),
            pltpu.VMEM((1, 1, segs), f32),
            pltpu.VMEM((n * nc - 1, 1, segs), f32),
            dma((len(operands),)), dma((h,)), dma((h,)), dma((1,)), dma((1,)), dma((h,)), dma((h,)), dma((h,)), dma((h,)), dma((2,)), dma((2,)), dma((2, h)), dma((2, h // rows)), dma((1,)), dma((1,)),
        ],
        compiler_params=pltpu.CompilerParams(
            collective_id=0, has_side_effects=True, vmem_limit_bytes=48 * 1024 * 1024
        ),
    )(*operands)
    return grad.reshape(cotangent.shape), gain.reshape(SEG_DEV)


def solution(mesh):
    in_specs = (
        P("axial", None, "cross", None),
        P("axial", None, None),
        P("axial", None),
        P("axial", None),
        P(),
        P(),
        P(),
        P("axial", "cross"),
    )
    out_specs = (P("axial", None, "cross", None), P(("axial", "cross")))
    return jax.shard_map(
        functools.partial(per_device, mesh.shape["axial"], mesh.shape["cross"]),
        mesh=mesh, in_specs=in_specs, out_specs=out_specs, check_vma=False,
    )
```

```python
import functools

import jax
import jax.numpy as jnp
from jax import lax
from jax.experimental import pallas as pl
from jax.experimental.pallas import tpu as pltpu
from jax.sharding import PartitionSpec as P

SEG_DEV = 4
EARLY = 2
MESH = pl.DeviceIdType.MESH
exact = lax.Precision.HIGHEST


def dot(a, b):
    return jnp.dot(a, b, precision=exact, preferred_element_type=jnp.float32)


def halves(x):
    high = x.astype(jnp.bfloat16)
    return high, (x - high.astype(jnp.float32)).astype(jnp.bfloat16)


def dot_halves(a, b):
    (ah, al), (bh, bl) = a, b
    one = functools.partial(jnp.dot, preferred_element_type=jnp.float32)
    return one(ah, bh) + (one(ah, bl) + one(al, bh))


def dot_split(a, b):
    return dot_halves(a, halves(b))


def dot3(a, b):
    return dot_halves(halves(a), halves(b))


def dot_split_b(a, b):
    return dot_halves(halves(a), b)


def spread(x, k, nb):
    packs, height, width = x.shape
    flat = x.reshape(packs * height, width)
    lane = lax.broadcasted_iota(jnp.int32, flat.shape, 1)
    return jnp.take_along_axis(flat, lane // nb * nb + k, axis=1).reshape(x.shape)


def invert_packs(a, nb, by_two=False):
    packs, _, width = a.shape
    row_id = lax.broadcasted_iota(jnp.int32, (packs, 8, width), 1)
    for first in range(0, nb, 8):
        home = a[:, first : first + 8]
        rest = [x for x in (a[:, :first], a[:, first + 8 :]) if x.shape[1]]
        rest = jnp.concatenate(rest, axis=1) if len(rest) > 1 else rest[0]
        near = [spread(home, first + j, nb) for j in range(8)]
        far = [spread(rest, first + j, nb) for j in range(8)]
        at = lax.broadcasted_iota(jnp.int32, home.shape, 2) % nb - first
        home = jnp.where((at >= 0) & (at < 8), jnp.where(at == row_id, 1.0, 0.0), home)
        at = lax.broadcasted_iota(jnp.int32, rest.shape, 2) % nb - first
        rest = jnp.where((at >= 0) & (at < 8), 0.0, rest)
        for j in range(0, 8, 2) if by_two else ():
            pick = lambda x, i: jnp.broadcast_to(x[:, i : i + 1], home.shape)
            a00, a01, a10, a11 = pick(near[j], j), pick(near[j + 1], j), pick(near[j], j + 1), pick(near[j + 1], j + 1)
            pivot = 1.0 / (a00 * a11 - a01 * a10)
            a00, a01, a10, a11 = a11 * pivot, a01 * pivot, a10 * pivot, a00 * pivot
            first_col, second_col = near[j], near[j + 1]

            def step(x):
                x0, x1 = pick(x, j), pick(x, j + 1)
                y0, y1 = a00 * x0 - a01 * x1, a11 * x1 - a10 * x0
                done = x - (first_col * y0 + second_col * y1)
                return jnp.where(row_id == j, y0, jnp.where(row_id == j + 1, y1, done))

            home = step(home)
            for m in range(j + 2, 8):
                near[m] = step(near[m])
        for j in range(8) if not by_two else ():
            pivot = 1.0 / jnp.broadcast_to(near[j][:, j : j + 1], home.shape)
            row = jnp.broadcast_to(home[:, j : j + 1], home.shape) * pivot
            home = jnp.where(row_id == j, row, home - near[j] * row)
            for m in range(j + 1, 8):
                entry = jnp.broadcast_to(near[m][:, j : j + 1], home.shape) * pivot
                near[m] = jnp.where(row_id == j, entry, near[m] - near[j] * entry)
        for j in range(8):
            rest = rest - far[j] * home[:, j : j + 1]
        a = jnp.concatenate([x for x in (rest[:, :first], home, rest[:, first:]) if x.shape[1]], axis=1)
    return a


def invert(mats):
    nb = mats[0].shape[0]
    pack = 128 // nb
    padded = list(mats)
    while len(padded) % pack:
        padded.append(mats[len(padded) % len(mats)])
    packs = [jnp.concatenate(padded[i : i + pack], axis=1) for i in range(0, len(padded), pack)]
    done = invert_packs(jnp.stack(packs), nb, True)
    return [done[i // pack, :, i % pack * nb : (i % pack + 1) * nb] for i in range(len(mats))]


def kernel(n, nc, cot_hbm, diag_hbm, low_hbm, up_hbm, cross_hbm, prof_hbm, open_hbm, seg_hbm, out, out_seg, GH, GL, FH, FL,
           cot, diag, low, up, cross_rate, prof_rate, open_ref, seg, G, F, X, V, port_out, port_in, msg_out, msg_in, pair_out, pair_in, back_out, back_in, mark_out, mark_in,
           edge_in, gain_out, gain_in, s_in, s_port, r_port, s_pair, r_pair, s_msg, r_msg, s_back, r_back, s_hal, r_hal,
           s_edge, r_edge, s_gain, r_gain, s_mark, r_mark):
    pairs_in = [(cot_hbm, cot), (diag_hbm, diag), (low_hbm, low), (up_hbm, up), (cross_hbm, cross_rate), (prof_hbm, prof_rate),
                (open_hbm, open_ref), (seg_hbm, seg)]
    loads = [pltpu.make_async_copy(src, dst, s_in.at[i]) for i, (src, dst) in enumerate(pairs_in)]
    for i in (1, 0, 2, 3, 4, 5, 6, 7):
        loads[i].start()
    cells, nb = diag.shape[0], diag.shape[1]
    size = cells * nb
    rows = cot.shape[0] // size
    nz = cot.shape[1]
    a = lax.axis_index("axial")
    h = n // 2
    per = rows * nz // h
    is_left = a < h
    own = lax.rem(a, h)
    half_of = a - own
    partner = lax.rem(a + h, n)
    c = lax.axis_index("cross")
    has_lo = c > 0
    has_hi = c < nc - 1

    barrier = pltpu.get_barrier_semaphore()
    peers = [(i, j) for i in range(n) for j in range(nc) if i or j]
    for i, j in peers:
        pl.semaphore_signal(barrier, inc=1, device_id=(lax.rem(a + i, n), lax.rem(c + j, nc)), device_id_type=MESH)

    for i in range(2, 8):
        loads[i].wait()
    V[...] = jnp.zeros(V.shape, jnp.float32)
    V[0:cells, 0:nb] = low[...]
    V[cells : 2 * cells, 0:nb] = up[...]
    V[2 * cells : 2 * cells + 1, 0:nb] = cross_rate[...]
    V[2 * cells + 2 : 2 * cells + 2 + rows, 0:cells] = seg[...].astype(jnp.float32)
    V[...] = V[...].T
    low_col = [V[0:nb, j : j + 1] for j in range(cells)]
    up_col = [V[0:nb, cells + j : cells + j + 1] for j in range(cells)]
    cross_col = V[0:nb, 2 * cells : 2 * cells + 1]
    seg_col = [V[0:cells, 2 * cells + 2 + y : 2 * cells + 3 + y] for y in range(rows)]
    eye = (lax.broadcasted_iota(jnp.int32, (nb, nb), 0) == lax.broadcasted_iota(jnp.int32, (nb, nb), 1)).astype(jnp.float32)

    loads[1].wait()
    pack = 128 // nb
    inverses = invert_packs(
        jnp.stack([jnp.concatenate([diag[g * pack + i] for i in range(pack)], axis=1) for g in range(cells // pack)]), nb)
    tall = [inverses[g].T for g in range(cells // pack)]

    loads[0].wait()
    for y in range(rows):
        F[:, (y + 1) * nz : (y + 2) * nz] = cot[pl.ds(y, size, stride=rows), :]
    main = slice(nz, (rows + 1) * nz)

    pl.semaphore_wait(barrier, len(peers))

    def hal_copy(down):
        src = F.at[:, nz : 2 * nz] if down else F.at[:, rows * nz : (rows + 1) * nz]
        dst = F.at[:, (rows + 1) * nz : (rows + 2) * nz] if down else F.at[:, 0:nz]
        way = 0 if down else 1
        return pltpu.make_async_remote_copy(
            src_ref=src, dst_ref=dst, send_sem=s_hal.at[way], recv_sem=r_hal.at[way],
            device_id=(a, c - 1 if down else c + 1), device_id_type=MESH)

    each = h // rows
    sends_down = jnp.logical_and(has_lo, own < each)
    sends_up = jnp.logical_and(has_hi, own >= h - each)

    def edge_copy(down, off):
        way = 0 if down else 1
        slot = own if down else own - (h - each)
        peer = lax.rem(own + off, h)
        return pltpu.make_async_remote_copy(
            src_ref=back_out.at[peer], dst_ref=edge_in.at[way, slot], send_sem=s_edge.at[way, off], recv_sem=r_edge.at[way, slot],
            device_id=(half_of + peer, c - 1 if down else c + 1), device_id_type=MESH)

    def edge_wait(way):
        for e in range(each):
            pltpu.make_async_remote_copy(
                src_ref=back_out.at[e], dst_ref=edge_in.at[way, e], send_sem=s_edge.at[way, e], recv_sem=r_edge.at[way, e],
                device_id=(a, c + 1 if way == 0 else c - 1), device_id_type=MESH).wait_recv()

    @pl.when(has_lo)
    def _():
        hal_copy(True).start()

    @pl.when(has_hi)
    def _():
        hal_copy(False).start()

    @pl.when(jnp.logical_not(has_lo))
    def _():
        F[:, 0:nz] = jnp.zeros((size, nz), jnp.float32)

    @pl.when(jnp.logical_not(has_hi))
    def _():
        F[:, (rows + 1) * nz : (rows + 2) * nz] = jnp.zeros((size, nz), jnp.float32)

    FH[:, main], FL[:, main] = halves(F[:, main])

    groups = []
    for i in range(cells):
        one = tall[i // pack][i % pack * nb : (i % pack + 1) * nb]
        groups.append(jnp.concatenate([low_col[i] * one, up_col[i] * one], axis=0))
    levels = []
    while len(groups) > 1:
        pairs = [(groups[i], groups[i + 1]) for i in range(0, len(groups), 2)]
        width = groups[0].shape[1]
        none = jnp.zeros((nb, width), jnp.float32)
        meets = [dot(r[:, 0:nb], l[nb:]) for l, r in pairs]
        weights = invert([eye - k[:nb, width - nb :] for k in meets])
        level = [dot(w, jnp.concatenate([k[:nb], r[:nb]], axis=1)) for (l, r), k, w in zip(pairs, meets, weights)]
        groups = []
        for (l, r), k, p in zip(pairs, meets, level):
            base = jnp.concatenate([jnp.concatenate([l[:nb], none], axis=1), jnp.concatenate([k[nb:], r[nb:]], axis=1)], axis=0)
            groups.append(base + dot(jnp.concatenate([l[:nb, width - nb :], k[nb:, width - nb :]], axis=0), p))
        levels.append(level)

    ends = groups[0]
    ports = jnp.concatenate([ends[:, 0:nb], ends[:, size - nb : size]], axis=1)
    port_out[...] = jnp.concatenate([ports[:nb], ports[nb:]], axis=1)

    def port_copy(off):
        return pltpu.make_async_remote_copy(
            src_ref=port_out, dst_ref=port_in.at[own], send_sem=s_port.at[off], recv_sem=r_port.at[off],
            device_id=(half_of + lax.rem(own + off, h), c), device_id_type=MESH)

    def msg_copy(off):
        peer = lax.rem(own + off, h)
        return pltpu.make_async_remote_copy(
            src_ref=msg_out.at[peer], dst_ref=msg_in.at[own], send_sem=s_msg.at[off], recv_sem=r_msg.at[off],
            device_id=(half_of + peer, c), device_id_type=MESH)

    def pair_copy(which):
        rest = pl.ds(nb, nb // 4) if which == 0 else pl.ds(0, nb)
        return pltpu.make_async_remote_copy(
            src_ref=pair_out.at[rest], dst_ref=pair_in.at[rest], send_sem=s_pair.at[which], recv_sem=r_pair.at[which],
            device_id=(partner, c), device_id_type=MESH)

    def back_copy(off):
        peer = lax.rem(own + off, h)
        return pltpu.make_async_remote_copy(
            src_ref=back_out.at[peer], dst_ref=back_in.at[own], send_sem=s_back.at[off], recv_sem=r_back.at[off],
            device_id=(half_of + peer, c), device_id_type=MESH)

    for off in range(1, h):
        port_copy(off).start()
    port_in[own] = port_out[...]
    field = dot_split_b(ends, (FH[:, main], FL[:, main]))
    fill = [jnp.zeros((2 * nb, 128 - per), jnp.float32)] if per < 128 else []
    for e in range(h):
        msg_out[e] = jnp.concatenate([field[:, e * per : (e + 1) * per]] + fill, axis=1)
    for off in range(1, h):
        msg_copy(off).start()
    msg_in[own] = msg_out[own]

    G[...] = jnp.zeros(G.shape, jnp.float32)
    same = (lax.broadcasted_iota(jnp.int32, (128, 128), 0) // nb) == (lax.broadcasted_iota(jnp.int32, (128, 128), 1) // nb)
    for g in range(cells // pack):
        G[g * 128 : (g + 1) * 128, g * 128 : (g + 1) * 128] = jnp.where(same, jnp.concatenate([tall[g]] * pack, axis=1), 0.0)
    def grow(level):
        width = level[0].shape[1] // 2
        span = max(128, 2 * width)
        places = [(2 * i * width, (2 * i + 1) * width, 2 * i * width // span * span) for i in range(len(level))]
        lefts = []
        for (o, m, lo), p in zip(places, level):
            if span > 2 * width:
                blank = [jnp.zeros((nb, x), jnp.float32) for x in (o - lo, lo + span - o - 2 * width)]
                p = jnp.concatenate([x for x in (blank[0], p, blank[1]) if x.shape[1]], axis=1)
            lefts.append(G[o:m, lo : lo + span] + dot3(G[o:m, m - nb : m], p))
        for (o, m, lo), left in zip(places, lefts):
            G[m : m + width, lo : lo + span] += dot3(G[m : m + width, m : m + nb], up_col[m // nb - 1] * left[width - nb :])
            G[o:m, lo : lo + span] = left

    for level in levels[:EARLY]:
        grow(level)

    for off in range(1, h):
        port_copy(off).wait_recv()

    lane = lax.broadcasted_iota(jnp.int32, (1, 256), 1)
    keep_l = jnp.where((lane >= nb) & (lane < 2 * nb), 0.0, 1.0)
    keep_r = jnp.where(lane < nb, 0.0, 1.0)
    field_in = None
    groups = [(port_in[d][:, 0 : 2 * nb], port_in[d][:, 2 * nb :], None) for d in range(h)]
    blank = jnp.zeros((nb, 128 - 2 * nb), jnp.float32)
    while len(groups) > 1:
        pairs = [(groups[i], groups[i + 1]) for i in range(0, len(groups), 2)]
        meets = [dot(r[0][:, 0:nb], l[1][:, nb : 2 * nb]) for l, r in pairs]
        weights = invert([eye - k for k in meets])
        if field_in is None:
            for off in range(1, h):
                msg_copy(off).wait_recv()
            field_in = [msg_in[d] for d in range(h)]
            groups = [(jnp.concatenate([f, blank, x[:nb]], axis=1), jnp.concatenate([t, blank, x[nb:]], axis=1), None)
                      for (f, t, _), x in zip(groups, field_in)]
            pairs = [(groups[i], groups[i + 1]) for i in range(0, len(groups), 2)]
        rights = [jnp.concatenate(r[0:2] if r[2] is None else r, axis=0) for l, r in pairs]
        meets = [dot(r[:, 0:nb], l[1]) for (l, _), r in zip(pairs, rights)]
        flows = [dot(w, k[:nb] * keep_l + r[:nb] * keep_r) for r, k, w in zip(rights, meets, weights)]
        groups = []
        for (l, _), r, k, p in zip(pairs, rights, meets, flows):
            left = jnp.concatenate([l[0], l[1]] if l[2] is None else [l[0], l[2], l[1]], axis=0)
            base = jnp.concatenate([left * keep_l, k[nb:] * keep_l + r[nb:] * keep_r], axis=0)
            both = base + dot(jnp.concatenate([left[:, nb : 2 * nb], k[nb:, nb : 2 * nb]], axis=0), p)
            seam = left.shape[0]
            inner = [both[nb : seam - nb], p, both[seam - nb : seam], both[seam + nb :]]
            groups.append((both[:nb], both[seam : seam + nb], jnp.concatenate([x for x in inner if x.shape[0]], axis=0)))
    first, last, inner = groups[0]
    mine = jnp.where(is_left, last[:, nb : 2 * nb], first[:, 0:nb])
    mine_field = jnp.where(is_left, last[:, 128:], first[:, 128:])
    pair_out[nb:] = jnp.concatenate([mine[s * nb // 4 : (s + 1) * nb // 4] for s in range(4)], axis=1)
    pair_copy(0).start()
    pair_out[0:nb] = mine_field
    pair_copy(1).start()
    inner_port = jnp.where(is_left, inner[:, nb : 2 * nb], inner[:, 0:nb])
    inner_field = inner[:, 128:]

    for level in levels[EARLY:]:
        grow(level)
    GH[...], GL[...] = halves(G[...])
    sent = jnp.concatenate([prof_rate[...]] * cells, axis=1)
    home_cell = lax.broadcasted_iota(jnp.int32, (cells, size), 1) // nb == lax.broadcasted_iota(jnp.int32, (cells, size), 0)
    sent = dot_halves(halves(jnp.where(home_cell, sent, 0.0)), (GH[...], GL[...]))
    sent_all = sent
    sent = jnp.concatenate([sent[:, 0:nb], sent[:, size - nb : size]], axis=1)
    idle = jnp.zeros((cells, 127 - 2 * nb), jnp.float32)
    for e in range(h):
        mark_out[e] = jnp.concatenate([sent, seg_col[e // each], idle], axis=1)

    def mark_copy(off):
        peer = lax.rem(own + off, h)
        return pltpu.make_async_remote_copy(
            src_ref=mark_out.at[peer], dst_ref=mark_in.at[own], send_sem=s_mark.at[off], recv_sem=r_mark.at[off],
            device_id=(half_of + peer, c), device_id_type=MESH)

    for off in range(1, h):
        mark_copy(off).start()
    mark_in[own] = mark_out[own]
    emit = dot_split_b(sent_all, (FH[:, main], FL[:, main]))
    opens = []
    for y in range(-1, rows + 1):
        at = jnp.clip(c * rows + y, 0, nc * rows - 1)
        line = open_ref[pl.ds(at, 1), :].astype(jnp.float32)
        if y == -1:
            line = jnp.where(has_lo, line, 0.0)
        if y == rows:
            line = jnp.where(has_hi, line, 0.0)
        opens.append(line)

    segs = gain_out.shape[-1]
    seg_id = lax.broadcasted_iota(jnp.int32, (1, segs), 1)
    gain = jnp.zeros((8, segs), jnp.float32)
    for y in range(rows):
        given = jnp.sum(emit[:, y * nz : (y + 1) * nz] * opens[y + 1], axis=1, keepdims=True) * (1.0 / nz)
        picked = jnp.where(seg_col[y] == seg_id.astype(jnp.float32), given, 0.0)
        for i in range(cells // 8):
            gain = gain + picked[i * 8 : (i + 1) * 8]

    pair_copy(0).wait_recv()
    theirs = jnp.concatenate([pair_in[nb:][:, s * nb : (s + 1) * nb] for s in range(4)], axis=0)
    both = dot(theirs, jnp.concatenate([mine_field, mine], axis=1))
    weight = invert([eye - both[:, 128:]])[0]
    pair_copy(1).wait_recv()
    given = dot(weight, pair_in[0:nb] + both[:, :128])
    inner = inner_field + dot(inner_port, given)
    for d in range(h):
        back_out[d, 0:nb] = inner[(2 * d - 1) * nb : 2 * d * nb] if d > 0 else jnp.where(is_left, 0.0, given)
        back_out[d, nb:] = inner[2 * d * nb : (2 * d + 1) * nb] if d < h - 1 else jnp.where(is_left, given, 0.0)
    for off in range(1, h):
        back_copy(off).start()
    back_in[own] = back_out[own]

    @pl.when(sends_down)
    def _():
        for off in range(h):
            edge_copy(True, off).start()

    @pl.when(sends_up)
    def _():
        for off in range(h):
            edge_copy(False, off).start()

    line = open_ref[pl.ds(c * rows + own // each, 1), :].astype(jnp.float32)
    wide = line[:, 0:per]
    for q in range(1, each):
        wide = jnp.where(lax.rem(own, each) == q, line[:, q * per : (q + 1) * per], wide)
    for off in range(1, h):
        mark_copy(off).wait_recv()
    passed = [dot3(mark_in[d][:, 0 : 2 * nb], back_out[d])[:, 0:per] for d in range(h)]
    for d in range(h):
        given = jnp.sum(passed[d] * wide, axis=1, keepdims=True) * (1.0 / nz)
        picked = jnp.where(mark_in[d][:, 2 * nb : 2 * nb + 1] == seg_id.astype(jnp.float32), given, 0.0)
        for i in range(cells // 8):
            gain = gain + picked[i * 8 : (i + 1) * 8]
    gain_out[0] = jnp.sum(gain, axis=0, keepdims=True)

    def gain_copy(k):
        i, j = peers[k]
        return pltpu.make_async_remote_copy(
            src_ref=gain_out.at[0], dst_ref=gain_in.at[k], send_sem=s_gain.at[0], recv_sem=r_gain.at[0],
            device_id=(lax.rem(a + i, n), lax.rem(c + j, nc)), device_id_type=MESH)

    for k in range(len(peers)):
        gain_copy(k).start()


    half = rows * nz // 2
    for part in range(2):
        at = slice(nz + part * half, nz + (part + 1) * half)
        X[:, at] = dot_halves((GH[...], GL[...]), (FH[:, at], FL[:, at]))

    @pl.when(has_lo)
    def _():
        hal_copy(True).wait_send()
        hal_copy(False).wait_recv()

    @pl.when(has_hi)
    def _():
        hal_copy(False).wait_send()
        hal_copy(True).wait_recv()

    sides = dot_split((GH[...], GL[...]), jnp.concatenate([F[:, 0:nz], F[:, (rows + 1) * nz : (rows + 2) * nz]], axis=1))
    X[:, 0:nz] = sides[:, 0:nz]
    X[:, (rows + 1) * nz : (rows + 2) * nz] = sides[:, nz : 2 * nz]

    for off in range(1, h):
        back_copy(off).wait_recv()

    flux = []
    for y in range(rows):
        flux.append(jnp.concatenate([back_in[y * each + e][:, 0:per] for e in range(each)], axis=1))
    flux = halves(jnp.concatenate(flux, axis=1))
    gc = (jnp.concatenate([GH[:, 0:nb], GH[:, size - nb : size]], axis=1),
          jnp.concatenate([GL[:, 0:nb], GL[:, size - nb : size]], axis=1))
    X[:, main] += dot_halves(gc, flux)

    zlane = lax.broadcasted_iota(jnp.int32, (1, nz), 1)
    step_col = jnp.concatenate([cross_col] * 4, axis=0)
    block = 4 * nb
    for y in list(range(1, rows - 1)) + [0, rows - 1]:
        if y == 0:
                @pl.when(has_lo)
                def _():
                    edge_wait(1)
                    X[:, 0:nz] += dot_split(gc, jnp.concatenate([edge_in[1, e][:, 0:per] for e in range(each)], axis=1))

                @pl.when(has_hi)
                def _():
                    edge_wait(0)
                    X[:, (rows + 1) * nz : (rows + 2) * nz] += dot_split(
                        gc, jnp.concatenate([edge_in[0, e][:, 0:per] for e in range(each)], axis=1))

        here = opens[y + 1]
        before = jnp.where(zlane == 0, 0.0, pltpu.roll(here, 1, 1)) * here
        after = jnp.where(zlane == nz - 1, 0.0, pltpu.roll(here, nz - 1, 1)) * here
        above = opens[y] * here
        below = opens[y + 2] * here
        total = before + after + above + below
        for i in range(size // block):
            at = slice(i * block, (i + 1) * block)
            x = X[at, (y + 1) * nz : (y + 2) * nz]
            moved = (above * (X[at, y * nz : (y + 1) * nz] - x) + below * (X[at, (y + 2) * nz : (y + 3) * nz] - x)
                     + before * (pltpu.roll(x, 1, 1) - x) + after * (pltpu.roll(x, nz - 1, 1) - x))
            out[pl.ds(i * block * rows + y, block, stride=rows), :] = x + step_col * moved

    pltpu.make_async_copy(gain_in, gain_in, r_gain.at[0]).wait()
    gain = gain_out[0] + jnp.sum(gain_in[...], axis=0)
    held = out_seg.shape[1]
    held_id = lax.broadcasted_iota(jnp.int32, (1, held), 1)
    result = jnp.zeros((1, held), jnp.float32)
    for j in range(held):
        picked = jnp.sum(jnp.where(seg_id == (a * nc + c) * held + j, gain, 0.0), axis=1, keepdims=True)
        result = jnp.where(held_id == j, picked, result)
    out_seg[...] = result

    pltpu.make_async_copy(gain_in, gain_in, s_gain.at[0]).wait()

    @pl.when(sends_down)
    def _():
        for off in range(h):
            edge_copy(True, off).wait_send()

    @pl.when(sends_up)
    def _():
        for off in range(h):
            edge_copy(False, off).wait_send()

    pair_copy(0).wait_send()
    pair_copy(1).wait_send()
    for off in range(1, h):
        port_copy(off).wait_send()
        mark_copy(off).wait_send()
        msg_copy(off).wait_send()
        back_copy(off).wait_send()


def per_device(n, nc, cotangent, diag_blocks, lower_rates, upper_rates, cross_rate, bin_profile, open_cells, segment_ids):
    cells, nb, rows, nz = cotangent.shape
    size, h = cells * nb, n // 2
    segs = SEG_DEV * n * nc
    vmem = pl.BlockSpec(memory_space=pltpu.VMEM)
    hbm = pl.BlockSpec(memory_space=pltpu.HBM)
    dma = pltpu.SemaphoreType.DMA
    f32 = jnp.float32
    operands = (
        cotangent.reshape(size * rows, nz), diag_blocks, lower_rates, upper_rates,
        cross_rate.reshape(1, nb), bin_profile.reshape(1, nb), open_cells, segment_ids.T,
    )
    operands = [pltpu.with_memory_space_constraint(x, pltpu.HBM) for x in operands]
    grad, gain = pl.pallas_call(
        functools.partial(kernel, n, nc),
        out_shape=(pltpu.VMEM((size * rows, nz), f32), jax.ShapeDtypeStruct((1, SEG_DEV), f32)),
        in_specs=[hbm] * len(operands),
        out_specs=(vmem, vmem),
        scratch_shapes=[pltpu.VMEM((size, size), jnp.bfloat16)] * 2 + [pltpu.VMEM((size, rows * nz + 2 * nz), jnp.bfloat16)] * 2 + [pltpu.VMEM(x.shape, x.dtype) for x in operands] + [
            pltpu.VMEM((size, size), f32),
            pltpu.VMEM((size, (rows + 2) * nz), f32),
            pltpu.VMEM((size, (rows + 2) * nz), f32),
            pltpu.VMEM((128, 128), f32),
            pltpu.VMEM((nb, 128), f32),
            pltpu.VMEM((h, nb, 128), f32),
            pltpu.VMEM((h, 2 * nb, 128), f32),
            pltpu.VMEM((h, 2 * nb, 128), f32),
            pltpu.VMEM((nb + nb // 4, 128), f32),
            pltpu.VMEM((nb + nb // 4, 128), f32),
            pltpu.VMEM((h, 2 * nb, 128), f32),
            pltpu.VMEM((h, 2 * nb, 128), f32),
            pltpu.VMEM((h, cells, 128), f32),
            pltpu.VMEM((h, cells, 128), f32),
            pltpu.VMEM((2, h // rows, 2 * nb, 128), f32),
            pltpu.VMEM((1, 1, segs), f32),
            pltpu.VMEM((n * nc - 1, 1, segs), f32),
            dma((len(operands),)), dma((h,)), dma((h,)), dma((2,)), dma((2,)), dma((h,)), dma((h,)), dma((h,)), dma((h,)), dma((2,)), dma((2,)), dma((2, h)), dma((2, h // rows)), dma((1,)), dma((1,)), dma((h,)), dma((h,)),
        ],
        compiler_params=pltpu.CompilerParams(
            collective_id=0, has_side_effects=True, vmem_limit_bytes=48 * 1024 * 1024
        ),
    )(*operands)
    return grad.reshape(cotangent.shape), gain.reshape(SEG_DEV)


def solution(mesh):
    in_specs = (
        P("axial", None, "cross", None),
        P("axial", None, None),
        P("axial", None),
        P("axial", None),
        P(),
        P(),
        P(),
        P("axial", "cross"),
    )
    out_specs = (P("axial", None, "cross", None), P(("axial", "cross")))
    return jax.shard_map(
        functools.partial(per_device, mesh.shape["axial"], mesh.shape["cross"]),
        mesh=mesh, in_specs=in_specs, out_specs=out_specs, check_vma=False,
    )
```

```python
import functools

import jax
import jax.numpy as jnp
from jax import lax
from jax.experimental import pallas as pl
from jax.experimental.pallas import tpu as pltpu
from jax.sharding import PartitionSpec as P

SEG_DEV = 4
EARLY = 2
MESH = pl.DeviceIdType.MESH
exact = lax.Precision.HIGHEST


def dot(a, b):
    return jnp.dot(a, b, precision=exact, preferred_element_type=jnp.float32)


def halves(x):
    high = x.astype(jnp.bfloat16)
    return high, (x - high.astype(jnp.float32)).astype(jnp.bfloat16)


def dot_halves(a, b):
    (ah, al), (bh, bl) = a, b
    one = functools.partial(jnp.dot, preferred_element_type=jnp.float32)
    return one(ah, bh) + (one(ah, bl) + one(al, bh))


def dot_split(a, b):
    return dot_halves(a, halves(b))


def dot3(a, b):
    return dot_halves(halves(a), halves(b))


def dot_split_b(a, b):
    return dot_halves(halves(a), b)


def spread(x, k, nb):
    packs, height, width = x.shape
    flat = x.reshape(packs * height, width)
    lane = lax.broadcasted_iota(jnp.int32, flat.shape, 1)
    return jnp.take_along_axis(flat, lane // nb * nb + k, axis=1).reshape(x.shape)


def invert_packs(a, nb, by_two=False):
    packs, _, width = a.shape
    row_id = lax.broadcasted_iota(jnp.int32, (packs, 8, width), 1)
    for first in range(0, nb, 8):
        home = a[:, first : first + 8]
        rest = [x for x in (a[:, :first], a[:, first + 8 :]) if x.shape[1]]
        rest = jnp.concatenate(rest, axis=1) if len(rest) > 1 else rest[0]
        near = [spread(home, first + j, nb) for j in range(8)]
        far = [spread(rest, first + j, nb) for j in range(8)]
        at = lax.broadcasted_iota(jnp.int32, home.shape, 2) % nb - first
        home = jnp.where((at >= 0) & (at < 8), jnp.where(at == row_id, 1.0, 0.0), home)
        at = lax.broadcasted_iota(jnp.int32, rest.shape, 2) % nb - first
        rest = jnp.where((at >= 0) & (at < 8), 0.0, rest)
        for j in range(0, 8, 2) if by_two else ():
            pick = lambda x, i: jnp.broadcast_to(x[:, i : i + 1], home.shape)
            a00, a01, a10, a11 = pick(near[j], j), pick(near[j + 1], j), pick(near[j], j + 1), pick(near[j + 1], j + 1)
            pivot = 1.0 / (a00 * a11 - a01 * a10)
            a00, a01, a10, a11 = a11 * pivot, a01 * pivot, a10 * pivot, a00 * pivot
            first_col, second_col = near[j], near[j + 1]

            def step(x):
                x0, x1 = pick(x, j), pick(x, j + 1)
                y0, y1 = a00 * x0 - a01 * x1, a11 * x1 - a10 * x0
                done = x - (first_col * y0 + second_col * y1)
                return jnp.where(row_id == j, y0, jnp.where(row_id == j + 1, y1, done))

            home = step(home)
            for m in range(j + 2, 8):
                near[m] = step(near[m])
        for j in range(8) if not by_two else ():
            pivot = 1.0 / jnp.broadcast_to(near[j][:, j : j + 1], home.shape)
            row = jnp.broadcast_to(home[:, j : j + 1], home.shape) * pivot
            home = jnp.where(row_id == j, row, home - near[j] * row)
            for m in range(j + 1, 8):
                entry = jnp.broadcast_to(near[m][:, j : j + 1], home.shape) * pivot
                near[m] = jnp.where(row_id == j, entry, near[m] - near[j] * entry)
        for j in range(8):
            rest = rest - far[j] * home[:, j : j + 1]
        a = jnp.concatenate([x for x in (rest[:, :first], home, rest[:, first:]) if x.shape[1]], axis=1)
    return a


def invert(mats):
    nb = mats[0].shape[0]
    pack = 128 // nb
    padded = list(mats)
    while len(padded) % pack:
        padded.append(mats[len(padded) % len(mats)])
    packs = [jnp.concatenate(padded[i : i + pack], axis=1) for i in range(0, len(padded), pack)]
    done = invert_packs(jnp.stack(packs), nb, True)
    return [done[i // pack, :, i % pack * nb : (i % pack + 1) * nb] for i in range(len(mats))]


def kernel(n, nc, cot_hbm, diag_hbm, low_hbm, up_hbm, cross_hbm, prof_hbm, open_hbm, seg_hbm, out, out_seg, GH, GL, FH, FL,
           cot, diag, low, up, cross_rate, prof_rate, open_ref, seg, G, F, X, V, port_out, port_in, msg_out, msg_in, pair_out, pair_in, back_out, back_in, mark_out, mark_in,
           edge_in, gain_out, gain_in, s_in, s_port, r_port, s_pair, r_pair, s_msg, r_msg, s_back, r_back, s_hal, r_hal,
           s_edge, r_edge, s_gain, r_gain, s_mark, r_mark):
    pairs_in = [(cot_hbm, cot), (diag_hbm, diag), (low_hbm, low), (up_hbm, up), (cross_hbm, cross_rate), (prof_hbm, prof_rate),
                (open_hbm, open_ref), (seg_hbm, seg)]
    loads = [pltpu.make_async_copy(src, dst, s_in.at[i]) for i, (src, dst) in enumerate(pairs_in)]
    for i in (1, 2, 3, 4, 5, 6, 7, 0):
        loads[i].start()
    cells, nb = diag.shape[0], diag.shape[1]
    size = cells * nb
    rows = cot.shape[0] // size
    nz = cot.shape[1]
    a = lax.axis_index("axial")
    h = n // 2
    per = rows * nz // h
    is_left = a < h
    own = lax.rem(a, h)
    half_of = a - own
    partner = lax.rem(a + h, n)
    c = lax.axis_index("cross")
    has_lo = c > 0
    has_hi = c < nc - 1

    barrier = pltpu.get_barrier_semaphore()
    peers = [(i, j) for i in range(n) for j in range(nc) if i or j]
    for i, j in peers:
        pl.semaphore_signal(barrier, inc=1, device_id=(lax.rem(a + i, n), lax.rem(c + j, nc)), device_id_type=MESH)

    for i in range(2, 8):
        loads[i].wait()
    V[...] = jnp.zeros(V.shape, jnp.float32)
    V[0:cells, 0:nb] = low[...]
    V[cells : 2 * cells, 0:nb] = up[...]
    V[2 * cells : 2 * cells + 1, 0:nb] = cross_rate[...]
    V[2 * cells + 2 : 2 * cells + 2 + rows, 0:cells] = seg[...].astype(jnp.float32)
    V[...] = V[...].T
    low_col = [V[0:nb, j : j + 1] for j in range(cells)]
    up_col = [V[0:nb, cells + j : cells + j + 1] for j in range(cells)]
    cross_col = V[0:nb, 2 * cells : 2 * cells + 1]
    seg_col = [V[0:cells, 2 * cells + 2 + y : 2 * cells + 3 + y] for y in range(rows)]
    eye = (lax.broadcasted_iota(jnp.int32, (nb, nb), 0) == lax.broadcasted_iota(jnp.int32, (nb, nb), 1)).astype(jnp.float32)

    loads[1].wait()
    loads[0].wait()
    pack = 128 // nb
    inverses = invert_packs(
        jnp.stack([jnp.concatenate([diag[g * pack + i] for i in range(pack)], axis=1) for g in range(cells // pack)]), nb)
    tall = [inverses[g].T for g in range(cells // pack)]

    for y in range(rows):
        F[:, (y + 1) * nz : (y + 2) * nz] = cot[pl.ds(y, size, stride=rows), :]
    main = slice(nz, (rows + 1) * nz)
    FH[:, main], FL[:, main] = halves(F[:, main])

    pl.semaphore_wait(barrier, len(peers))

    def hal_copy(down):
        src = F.at[:, nz : 2 * nz] if down else F.at[:, rows * nz : (rows + 1) * nz]
        dst = F.at[:, (rows + 1) * nz : (rows + 2) * nz] if down else F.at[:, 0:nz]
        way = 0 if down else 1
        return pltpu.make_async_remote_copy(
            src_ref=src, dst_ref=dst, send_sem=s_hal.at[way], recv_sem=r_hal.at[way],
            device_id=(a, c - 1 if down else c + 1), device_id_type=MESH)

    each = h // rows
    sends_down = jnp.logical_and(has_lo, own < each)
    sends_up = jnp.logical_and(has_hi, own >= h - each)

    def edge_copy(down, off):
        way = 0 if down else 1
        slot = own if down else own - (h - each)
        peer = lax.rem(own + off, h)
        return pltpu.make_async_remote_copy(
            src_ref=back_out.at[peer], dst_ref=edge_in.at[way, slot], send_sem=s_edge.at[way, off], recv_sem=r_edge.at[way, slot],
            device_id=(half_of + peer, c - 1 if down else c + 1), device_id_type=MESH)

    def edge_wait(way):
        for e in range(each):
            pltpu.make_async_remote_copy(
                src_ref=back_out.at[e], dst_ref=edge_in.at[way, e], send_sem=s_edge.at[way, e], recv_sem=r_edge.at[way, e],
                device_id=(a, c + 1 if way == 0 else c - 1), device_id_type=MESH).wait_recv()

    @pl.when(has_lo)
    def _():
        hal_copy(True).start()

    @pl.when(has_hi)
    def _():
        hal_copy(False).start()

    @pl.when(jnp.logical_not(has_lo))
    def _():
        F[:, 0:nz] = jnp.zeros((size, nz), jnp.float32)

    @pl.when(jnp.logical_not(has_hi))
    def _():
        F[:, (rows + 1) * nz : (rows + 2) * nz] = jnp.zeros((size, nz), jnp.float32)


    groups = []
    for i in range(cells):
        one = tall[i // pack][i % pack * nb : (i % pack + 1) * nb]
        groups.append(jnp.concatenate([low_col[i] * one, up_col[i] * one], axis=0))
    levels = []
    while len(groups) > 1:
        pairs = [(groups[i], groups[i + 1]) for i in range(0, len(groups), 2)]
        width = groups[0].shape[1]
        none = jnp.zeros((nb, width), jnp.float32)
        meets = [dot(r[:, 0:nb], l[nb:]) for l, r in pairs]
        weights = invert([eye - k[:nb, width - nb :] for k in meets])
        level = [dot(w, jnp.concatenate([k[:nb], r[:nb]], axis=1)) for (l, r), k, w in zip(pairs, meets, weights)]
        groups = []
        for (l, r), k, p in zip(pairs, meets, level):
            base = jnp.concatenate([jnp.concatenate([l[:nb], none], axis=1), jnp.concatenate([k[nb:], r[nb:]], axis=1)], axis=0)
            groups.append(base + dot(jnp.concatenate([l[:nb, width - nb :], k[nb:, width - nb :]], axis=0), p))
        levels.append(level)

    ends = groups[0]
    ports = jnp.concatenate([ends[:, 0:nb], ends[:, size - nb : size]], axis=1)
    port_out[...] = jnp.concatenate([ports[:nb], ports[nb:]], axis=1)

    def port_copy(off):
        return pltpu.make_async_remote_copy(
            src_ref=port_out, dst_ref=port_in.at[own], send_sem=s_port.at[off], recv_sem=r_port.at[off],
            device_id=(half_of + lax.rem(own + off, h), c), device_id_type=MESH)

    def msg_copy(off):
        peer = lax.rem(own + off, h)
        return pltpu.make_async_remote_copy(
            src_ref=msg_out.at[peer], dst_ref=msg_in.at[own], send_sem=s_msg.at[off], recv_sem=r_msg.at[off],
            device_id=(half_of + peer, c), device_id_type=MESH)

    def pair_copy(which):
        rest = pl.ds(nb, nb // 4) if which == 0 else pl.ds(0, nb)
        return pltpu.make_async_remote_copy(
            src_ref=pair_out.at[rest], dst_ref=pair_in.at[rest], send_sem=s_pair.at[which], recv_sem=r_pair.at[which],
            device_id=(partner, c), device_id_type=MESH)

    def back_copy(off):
        peer = lax.rem(own + off, h)
        return pltpu.make_async_remote_copy(
            src_ref=back_out.at[peer], dst_ref=back_in.at[own], send_sem=s_back.at[off], recv_sem=r_back.at[off],
            device_id=(half_of + peer, c), device_id_type=MESH)

    for off in range(1, h):
        port_copy(off).start()
    port_in[own] = port_out[...]
    field = dot_split_b(ends, (FH[:, main], FL[:, main]))
    fill = [jnp.zeros((2 * nb, 128 - per), jnp.float32)] if per < 128 else []
    for e in range(h):
        msg_out[e] = jnp.concatenate([field[:, e * per : (e + 1) * per]] + fill, axis=1)
    for off in range(1, h):
        msg_copy(off).start()
    msg_in[own] = msg_out[own]

    G[...] = jnp.zeros(G.shape, jnp.float32)
    same = (lax.broadcasted_iota(jnp.int32, (128, 128), 0) // nb) == (lax.broadcasted_iota(jnp.int32, (128, 128), 1) // nb)
    for g in range(cells // pack):
        G[g * 128 : (g + 1) * 128, g * 128 : (g + 1) * 128] = jnp.where(same, jnp.concatenate([tall[g]] * pack, axis=1), 0.0)
    def grow(level):
        width = level[0].shape[1] // 2
        span = max(128, 2 * width)
        places = [(2 * i * width, (2 * i + 1) * width, 2 * i * width // span * span) for i in range(len(level))]
        lefts = []
        for (o, m, lo), p in zip(places, level):
            if span > 2 * width:
                blank = [jnp.zeros((nb, x), jnp.float32) for x in (o - lo, lo + span - o - 2 * width)]
                p = jnp.concatenate([x for x in (blank[0], p, blank[1]) if x.shape[1]], axis=1)
            lefts.append(G[o:m, lo : lo + span] + dot3(G[o:m, m - nb : m], p))
        for (o, m, lo), left in zip(places, lefts):
            G[m : m + width, lo : lo + span] += dot3(G[m : m + width, m : m + nb], up_col[m // nb - 1] * left[width - nb :])
            G[o:m, lo : lo + span] = left

    for level in levels[:EARLY]:
        grow(level)

    for off in range(1, h):
        port_copy(off).wait_recv()

    lane = lax.broadcasted_iota(jnp.int32, (1, 256), 1)
    keep_l = jnp.where((lane >= nb) & (lane < 2 * nb), 0.0, 1.0)
    keep_r = jnp.where(lane < nb, 0.0, 1.0)
    field_in = None
    groups = [(port_in[d][:, 0 : 2 * nb], port_in[d][:, 2 * nb :], None) for d in range(h)]
    blank = jnp.zeros((nb, 128 - 2 * nb), jnp.float32)
    while len(groups) > 1:
        pairs = [(groups[i], groups[i + 1]) for i in range(0, len(groups), 2)]
        meets = [dot(r[0][:, 0:nb], l[1][:, nb : 2 * nb]) for l, r in pairs]
        weights = invert([eye - k for k in meets])
        if field_in is None:
            for off in range(1, h):
                msg_copy(off).wait_recv()
            field_in = [msg_in[d] for d in range(h)]
            groups = [(jnp.concatenate([f, blank, x[:nb]], axis=1), jnp.concatenate([t, blank, x[nb:]], axis=1), None)
                      for (f, t, _), x in zip(groups, field_in)]
            pairs = [(groups[i], groups[i + 1]) for i in range(0, len(groups), 2)]
        rights = [jnp.concatenate(r[0:2] if r[2] is None else r, axis=0) for l, r in pairs]
        meets = [dot(r[:, 0:nb], l[1]) for (l, _), r in zip(pairs, rights)]
        flows = [dot(w, k[:nb] * keep_l + r[:nb] * keep_r) for r, k, w in zip(rights, meets, weights)]
        groups = []
        for (l, _), r, k, p in zip(pairs, rights, meets, flows):
            left = jnp.concatenate([l[0], l[1]] if l[2] is None else [l[0], l[2], l[1]], axis=0)
            base = jnp.concatenate([left * keep_l, k[nb:] * keep_l + r[nb:] * keep_r], axis=0)
            both = base + dot(jnp.concatenate([left[:, nb : 2 * nb], k[nb:, nb : 2 * nb]], axis=0), p)
            seam = left.shape[0]
            inner = [both[nb : seam - nb], p, both[seam - nb : seam], both[seam + nb :]]
            groups.append((both[:nb], both[seam : seam + nb], jnp.concatenate([x for x in inner if x.shape[0]], axis=0)))
    first, last, inner = groups[0]
    mine = jnp.where(is_left, last[:, nb : 2 * nb], first[:, 0:nb])
    mine_field = jnp.where(is_left, last[:, 128:], first[:, 128:])
    pair_out[nb:] = jnp.concatenate([mine[s * nb // 4 : (s + 1) * nb // 4] for s in range(4)], axis=1)
    pair_copy(0).start()
    pair_out[0:nb] = mine_field
    pair_copy(1).start()
    inner_port = jnp.where(is_left, inner[:, nb : 2 * nb], inner[:, 0:nb])
    inner_field = inner[:, 128:]

    for level in levels[EARLY:]:
        grow(level)
    GH[...], GL[...] = halves(G[...])
    sent = jnp.concatenate([prof_rate[...]] * cells, axis=1)
    home_cell = lax.broadcasted_iota(jnp.int32, (cells, size), 1) // nb == lax.broadcasted_iota(jnp.int32, (cells, size), 0)
    sent = dot_halves(halves(jnp.where(home_cell, sent, 0.0)), (GH[...], GL[...]))
    sent_all = sent
    sent = jnp.concatenate([sent[:, 0:nb], sent[:, size - nb : size]], axis=1)
    idle = jnp.zeros((cells, 127 - 2 * nb), jnp.float32)
    for e in range(h):
        mark_out[e] = jnp.concatenate([sent, seg_col[e // each], idle], axis=1)

    def mark_copy(off):
        peer = lax.rem(own + off, h)
        return pltpu.make_async_remote_copy(
            src_ref=mark_out.at[peer], dst_ref=mark_in.at[own], send_sem=s_mark.at[off], recv_sem=r_mark.at[off],
            device_id=(half_of + peer, c), device_id_type=MESH)

    for off in range(1, h):
        mark_copy(off).start()
    mark_in[own] = mark_out[own]
    emit = dot_split_b(sent_all, (FH[:, main], FL[:, main]))
    opens = []
    for y in range(-1, rows + 1):
        at = jnp.clip(c * rows + y, 0, nc * rows - 1)
        line = open_ref[pl.ds(at, 1), :].astype(jnp.float32)
        if y == -1:
            line = jnp.where(has_lo, line, 0.0)
        if y == rows:
            line = jnp.where(has_hi, line, 0.0)
        opens.append(line)

    segs = gain_out.shape[-1]
    seg_id = lax.broadcasted_iota(jnp.int32, (1, segs), 1)
    gain = jnp.zeros((8, segs), jnp.float32)
    for y in range(rows):
        given = jnp.sum(emit[:, y * nz : (y + 1) * nz] * opens[y + 1], axis=1, keepdims=True) * (1.0 / nz)
        picked = jnp.where(seg_col[y] == seg_id.astype(jnp.float32), given, 0.0)
        for i in range(cells // 8):
            gain = gain + picked[i * 8 : (i + 1) * 8]

    half = rows * nz // 2
    for part in range(2):
        at = slice(nz + part * half, nz + (part + 1) * half)
        X[:, at] = dot_halves((GH[...], GL[...]), (FH[:, at], FL[:, at]))

    pair_copy(0).wait_recv()
    theirs = jnp.concatenate([pair_in[nb:][:, s * nb : (s + 1) * nb] for s in range(4)], axis=0)
    both = dot(theirs, jnp.concatenate([mine_field, mine], axis=1))
    weight = invert([eye - both[:, 128:]])[0]
    pair_copy(1).wait_recv()
    given = dot(weight, pair_in[0:nb] + both[:, :128])
    inner = inner_field + dot(inner_port, given)
    for d in range(h):
        back_out[d, 0:nb] = inner[(2 * d - 1) * nb : 2 * d * nb] if d > 0 else jnp.where(is_left, 0.0, given)
        back_out[d, nb:] = inner[2 * d * nb : (2 * d + 1) * nb] if d < h - 1 else jnp.where(is_left, given, 0.0)
    @pl.when(sends_down)
    def _():
        for off in range(h):
            edge_copy(True, off).start()

    @pl.when(sends_up)
    def _():
        for off in range(h):
            edge_copy(False, off).start()

    for off in range(1, h):
        back_copy(off).start()
    back_in[own] = back_out[own]


    line = open_ref[pl.ds(c * rows + own // each, 1), :].astype(jnp.float32)
    wide = line[:, 0:per]
    for q in range(1, each):
        wide = jnp.where(lax.rem(own, each) == q, line[:, q * per : (q + 1) * per], wide)
    for off in range(1, h):
        mark_copy(off).wait_recv()
    passed = [dot3(mark_in[d][:, 0 : 2 * nb], back_out[d])[:, 0:per] for d in range(h)]
    for d in range(h):
        given = jnp.sum(passed[d] * wide, axis=1, keepdims=True) * (1.0 / nz)
        picked = jnp.where(mark_in[d][:, 2 * nb : 2 * nb + 1] == seg_id.astype(jnp.float32), given, 0.0)
        for i in range(cells // 8):
            gain = gain + picked[i * 8 : (i + 1) * 8]
    gain_out[0] = jnp.sum(gain, axis=0, keepdims=True)

    def gain_copy(k):
        i, j = peers[k]
        return pltpu.make_async_remote_copy(
            src_ref=gain_out.at[0], dst_ref=gain_in.at[k], send_sem=s_gain.at[0], recv_sem=r_gain.at[0],
            device_id=(lax.rem(a + i, n), lax.rem(c + j, nc)), device_id_type=MESH)

    for k in range(len(peers)):
        gain_copy(k).start()


    @pl.when(has_lo)
    def _():
        hal_copy(True).wait_send()
        hal_copy(False).wait_recv()

    @pl.when(has_hi)
    def _():
        hal_copy(False).wait_send()
        hal_copy(True).wait_recv()

    sides = dot_split((GH[...], GL[...]), jnp.concatenate([F[:, 0:nz], F[:, (rows + 1) * nz : (rows + 2) * nz]], axis=1))
    X[:, 0:nz] = sides[:, 0:nz]
    X[:, (rows + 1) * nz : (rows + 2) * nz] = sides[:, nz : 2 * nz]

    high = [GH[:, 0:nb], GH[:, size - nb : size]]
    reply = jnp.concatenate(high * 2 + [GL[:, 0:nb], GL[:, size - nb : size]], axis=1)

    def respond(x):
        x, small = halves(x)
        return jnp.dot(reply, jnp.concatenate([x, small, x], axis=0), preferred_element_type=jnp.float32)

    for off in range(1, h):
        back_copy(off).wait_recv()

    flux = []
    for y in range(rows):
        flux.append(jnp.concatenate([back_in[y * each + e][:, 0:per] for e in range(each)], axis=1))
    X[:, main] += respond(jnp.concatenate(flux, axis=1))

    zlane = lax.broadcasted_iota(jnp.int32, (1, nz), 1)
    step_col = jnp.concatenate([cross_col] * 4, axis=0)
    block = 4 * nb
    for y in list(range(1, rows - 1)) + [0, rows - 1]:
        if y == 0:
                @pl.when(has_lo)
                def _():
                    edge_wait(1)
                    X[:, 0:nz] += respond(jnp.concatenate([edge_in[1, e][:, 0:per] for e in range(each)], axis=1))

                @pl.when(has_hi)
                def _():
                    edge_wait(0)
                    X[:, (rows + 1) * nz : (rows + 2) * nz] += respond(
                        jnp.concatenate([edge_in[0, e][:, 0:per] for e in range(each)], axis=1))

        here = opens[y + 1]
        before = jnp.where(zlane == 0, 0.0, pltpu.roll(here, 1, 1)) * here
        after = jnp.where(zlane == nz - 1, 0.0, pltpu.roll(here, nz - 1, 1)) * here
        above = opens[y] * here
        below = opens[y + 2] * here
        total = before + after + above + below
        for i in range(size // block):
            at = slice(i * block, (i + 1) * block)
            x = X[at, (y + 1) * nz : (y + 2) * nz]
            moved = (above * (X[at, y * nz : (y + 1) * nz] - x) + below * (X[at, (y + 2) * nz : (y + 3) * nz] - x)
                     + before * (pltpu.roll(x, 1, 1) - x) + after * (pltpu.roll(x, nz - 1, 1) - x))
            out[pl.ds(i * block * rows + y, block, stride=rows), :] = x + step_col * moved

    pltpu.make_async_copy(gain_in, gain_in, r_gain.at[0]).wait()
    gain = gain_out[0] + jnp.sum(gain_in[...], axis=0)
    held = out_seg.shape[1]
    held_id = lax.broadcasted_iota(jnp.int32, (1, held), 1)
    result = jnp.zeros((1, held), jnp.float32)
    for j in range(held):
        picked = jnp.sum(jnp.where(seg_id == (a * nc + c) * held + j, gain, 0.0), axis=1, keepdims=True)
        result = jnp.where(held_id == j, picked, result)
    out_seg[...] = result

    pltpu.make_async_copy(gain_in, gain_in, s_gain.at[0]).wait()

    @pl.when(sends_down)
    def _():
        for off in range(h):
            edge_copy(True, off).wait_send()

    @pl.when(sends_up)
    def _():
        for off in range(h):
            edge_copy(False, off).wait_send()

    pair_copy(0).wait_send()
    pair_copy(1).wait_send()
    for off in range(1, h):
        port_copy(off).wait_send()
        mark_copy(off).wait_send()
        msg_copy(off).wait_send()
        back_copy(off).wait_send()


def per_device(n, nc, cotangent, diag_blocks, lower_rates, upper_rates, cross_rate, bin_profile, open_cells, segment_ids):
    cells, nb, rows, nz = cotangent.shape
    size, h = cells * nb, n // 2
    segs = SEG_DEV * n * nc
    vmem = pl.BlockSpec(memory_space=pltpu.VMEM)
    hbm = pl.BlockSpec(memory_space=pltpu.HBM)
    dma = pltpu.SemaphoreType.DMA
    f32 = jnp.float32
    operands = (
        cotangent.reshape(size * rows, nz), diag_blocks, lower_rates, upper_rates,
        cross_rate.reshape(1, nb), bin_profile.reshape(1, nb), open_cells, segment_ids.T,
    )
    operands = [pltpu.with_memory_space_constraint(x, pltpu.HBM) for x in operands]
    grad, gain = pl.pallas_call(
        functools.partial(kernel, n, nc),
        out_shape=(pltpu.VMEM((size * rows, nz), f32), jax.ShapeDtypeStruct((1, SEG_DEV), f32)),
        in_specs=[hbm] * len(operands),
        out_specs=(vmem, vmem),
        scratch_shapes=[pltpu.VMEM((size, size), jnp.bfloat16)] * 2 + [pltpu.VMEM((size, rows * nz + 2 * nz), jnp.bfloat16)] * 2 + [pltpu.VMEM(x.shape, x.dtype) for x in operands] + [
            pltpu.VMEM((size, size), f32),
            pltpu.VMEM((size, (rows + 2) * nz), f32),
            pltpu.VMEM((size, (rows + 2) * nz), f32),
            pltpu.VMEM((128, 128), f32),
            pltpu.VMEM((nb, 128), f32),
            pltpu.VMEM((h, nb, 128), f32),
            pltpu.VMEM((h, 2 * nb, 128), f32),
            pltpu.VMEM((h, 2 * nb, 128), f32),
            pltpu.VMEM((nb + nb // 4, 128), f32),
            pltpu.VMEM((nb + nb // 4, 128), f32),
            pltpu.VMEM((h, 2 * nb, 128), f32),
            pltpu.VMEM((h, 2 * nb, 128), f32),
            pltpu.VMEM((h, cells, 128), f32),
            pltpu.VMEM((h, cells, 128), f32),
            pltpu.VMEM((2, h // rows, 2 * nb, 128), f32),
            pltpu.VMEM((1, 1, segs), f32),
            pltpu.VMEM((n * nc - 1, 1, segs), f32),
            dma((len(operands),)), dma((h,)), dma((h,)), dma((2,)), dma((2,)), dma((h,)), dma((h,)), dma((h,)), dma((h,)), dma((2,)), dma((2,)), dma((2, h)), dma((2, h // rows)), dma((1,)), dma((1,)), dma((h,)), dma((h,)),
        ],
        compiler_params=pltpu.CompilerParams(
            collective_id=0, has_side_effects=True, vmem_limit_bytes=48 * 1024 * 1024
        ),
    )(*operands)
    return grad.reshape(cotangent.shape), gain.reshape(SEG_DEV)


def solution(mesh):
    in_specs = (
        P("axial", None, "cross", None),
        P("axial", None, None),
        P("axial", None),
        P("axial", None),
        P(),
        P(),
        P(),
        P("axial", "cross"),
    )
    out_specs = (P("axial", None, "cross", None), P(("axial", "cross")))
    return jax.shard_map(
        functools.partial(per_device, mesh.shape["axial"], mesh.shape["cross"]),
        mesh=mesh, in_specs=in_specs, out_specs=out_specs, check_vma=False,
    )
```
